128 devices in a mesh: fibre: 4 (over x), tm: 4 (over z_hi, core), rep: 8 (over z_lo, y).
Axes of the slice: x: 4, y: 4, z: 4 (z_hi: 2, z_lo: 2; z = z_hi * 2 + z_lo), core: 2. Of those that a mesh axis runs over, the one named last changes fastest.
Arguments:
- records: bfloat16 [8, 64, 2048, 128], P('rep', 'fibre', 'tm'), may hold values from -6 to 6
- time_weight: bfloat16 [9, 128, 128], replicated, may hold values from -0.1875 to 0.1875
- fibre_weight: bfloat16 [9, 128, 128], replicated, may hold values from -0.1875 to 0.1875
- cotangent: bfloat16 [8, 64, 2048, 128], P('rep', 'fibre', 'tm'), may hold values from -6 to 6
Outputs:
- mixed: bfloat16 [8, 64, 2048, 128], P('rep', 'fibre', 'tm')
- d_records: bfloat16 [8, 64, 2048, 128], P('rep', 'fibre', 'tm')
- grad_time: float32 [9, 128, 128], replicated
- grad_fibre: float32 [9, 128, 128], replicated
The draws below stay inside these ranges and needn't reach their ends.
All inputs are finite; a program needn't handle non-finite values.
Results may differ from the reference program's by a relative error of at most 0.0032.
Values may be sent and summed in bfloat16 or wider, within the bound.
A program may use at most 256 MiB of HBM per device.

```python
import jax
import jax.numpy as jnp
from jax import lax

C = 128
TAPS = 9
NF = 64
NT = 2048
RECORDS = 8


def shard_levels(own_key, dims, shards, smallest, high):
    def one(axis_at, blocks):
        steps = jax.random.uniform(jax.random.fold_in(jax.random.fold_in(own_key, 6), axis_at), (blocks,), jnp.float32, smallest / len(shards), high / len(shards))
        return jnp.repeat(jnp.exp(steps), dims[axis_at] // blocks).reshape((-1,) + (1,) * (len(dims) - axis_at - 1))

    loudness = one(*shards[0])
    for cut in shards[1:]:
        loudness = loudness * one(*cut)
    return loudness


def noise(stream_key, extent, scale, bound, split=(), kind=jnp.bfloat16):
    array = jax.random.normal(stream_key, extent, jnp.float32) * scale
    if len(split) > 0:
        array = shard_levels(stream_key, extent, split, -0.22, 0.18) * array
    return jnp.clip(array, min=-bound, max=bound).astype(kind)


def setup_inputs(seed: int = 0) -> dict:
    streams_of = jax.random.split(jax.random.key(seed), 5)
    return {
        "records": noise(streams_of[0], (RECORDS, NF, NT, C), 1.0, 6.0, ((0, 8), (1, 4), (2, 4))),
        "time_weight": noise(streams_of[1], (TAPS, C, C), (TAPS * C) ** -0.5, 0.1875),
        "fibre_weight": noise(streams_of[2], (TAPS, C, C), (TAPS * C) ** -0.5, 0.1875),
        "cotangent": noise(streams_of[3], (RECORDS, NF, NT, C), 1.0, 6.0, ((0, 8), (1, 4), (2, 4))),
    }


def time_pad(field):
    return jnp.pad(field, ((0, 0), (32, 32), (0, 0)))

def fibre_pad(field):
    return jnp.pad(field, ((4, 4), (0, 0), (0, 0)))

def time_slice(padded, k):
    return padded[:, 8 * k:8 * k + NT, :]

def fibre_slice(padded, k):
    return padded[k:k + NF, :, :]

def apply_conv(padded, weight, slicer):
    width = weight.shape[1]
    total = jnp.zeros((NF * NT, weight.shape[2]), jnp.float32)
    for k in range(9):
        piece = slicer(padded, k).reshape(-1, width)
        total = total + jnp.dot(piece, weight[k], preferred_element_type=jnp.float32)
    return total.reshape(NF, NT, -1)

def weight_grad(padded, right, slicer):
    width = right.shape[-1]
    flat = right.reshape(-1, width)
    parts = []
    for k in range(9):
        piece = slicer(padded, k).reshape(-1, width)
        parts.append(jnp.dot(piece.T, flat, preferred_element_type=jnp.float32))
    return jnp.stack(parts)

def one_record(args):
    record, cot, time_weight, fibre_weight = args
    flip_time = jnp.transpose(time_weight[::-1], (0, 2, 1))
    flip_fibre = jnp.transpose(fibre_weight[::-1], (0, 2, 1))
    x_pad = time_pad(record)
    pre = apply_conv(x_pad, time_weight, time_slice)
    sig = jax.nn.sigmoid(pre)
    hidden = (pre * sig).astype(jnp.bfloat16)
    h_pad = fibre_pad(hidden)
    mixed = (record.astype(jnp.float32) + apply_conv(h_pad, fibre_weight, fibre_slice)).astype(jnp.bfloat16)
    g_pad = fibre_pad(cot)
    d_hidden = apply_conv(g_pad, flip_fibre, fibre_slice)
    d_pre = (d_hidden * sig * (1.0 + pre * (1.0 - sig))).astype(jnp.bfloat16)
    da_pad = time_pad(d_pre)
    d_rec = (cot.astype(jnp.float32) + apply_conv(da_pad, flip_time, time_slice)).astype(jnp.bfloat16)
    grad_f = weight_grad(h_pad, cot, fibre_slice)
    grad_t = weight_grad(x_pad, d_pre, time_slice)
    return (mixed, d_rec, grad_t, grad_f)

def reference(records, time_weight, fibre_weight, cotangent):
    count = records.shape[0]
    tw = jnp.broadcast_to(time_weight, (count,) + time_weight.shape)
    fw = jnp.broadcast_to(fibre_weight, (count,) + fibre_weight.shape)
    mixed, d_rec, grad_t, grad_f = lax.map(one_record, (records, cotangent, tw, fw))
    factor = 1.0 / jnp.sqrt(jnp.float32(RECORDS * NF * NT))
    return (mixed, d_rec, lax.optimization_barrier(jnp.sum(grad_t, axis=0)) * factor, lax.optimization_barrier(jnp.sum(grad_f, axis=0)) * factor)
```

```python
import functools

import jax
import jax.numpy as jnp
from jax import lax
from jax.experimental import pallas as pl
from jax.experimental.pallas import tpu as pltpu
from jax.sharding import PartitionSpec as P

MESH = pl.DeviceIdType.MESH
BF, F32 = jnp.bfloat16, jnp.float32
TILE = 4
UNROLL = 2
CHUNKS = 4


def dot(a, b):
    return jnp.dot(a, b, preferred_element_type=F32)


def loop(low, high, body):
    lax.fori_loop(low, high, lambda i, c: (body(i), c)[1], 0, unroll=min(UNROLL, high - low))


def aligned(index, size):
    return pl.ds(pl.multiple_of(index * size, size), size)


def pair_weights(dst, block):
    zero = jnp.zeros((128, 128), BF)
    for b in range(5):
        top, low = slice(256 * b, 256 * b + 128), slice(256 * b + 128, 256 * b + 256)
        dst[top, 0:128] = block(2 * b)
        dst[top, 128:256] = block(2 * b - 1) if b > 0 else zero
        dst[low, 0:128] = block(2 * b + 1) if b < 4 else zero
        dst[low, 128:256] = block(2 * b)


def to_time_pairs(src, q):
    v = src[:, aligned(q, 16), :].astype(F32)
    lo, hi = v[:, 0:8].reshape(128, 128), v[:, 8:16].reshape(128, 128)
    return jnp.concatenate([lo, hi], axis=1).astype(BF)


def natural(y):
    y = y.reshape(16, 8, 256)
    return jnp.concatenate([y[:, :, :128], y[:, :, 128:]], axis=1)


def time_conv(src, w, q0):
    lhs = [src[pl.ds(q0 + b, TILE)].reshape(TILE * 128, 256) for b in range(5)]
    return dot(jnp.concatenate(lhs, axis=1), w[...])


def fibre_conv(src, w, pair, at):
    v = src[pl.ds(2 * pair, 10), at, :]
    return dot(jnp.concatenate([v[i] for i in range(10)], axis=1), w[...])


def do_hidden(xt, w, h, slope, q0):
    y = time_conv(xt, w, q0)
    s = 0.5 * jnp.tanh(0.5 * y) + 0.5
    hid = y * s
    slope[pl.ds(q0, TILE)] = (s + hid * (1.0 - s)).reshape(TILE, 128, 256)
    for j in range(TILE):
        h[4:20, aligned(q0 + j, 16), :] = natural(hid[128 * j : 128 * j + 128]).astype(BF)


def do_d_pre(g, w, slope, dp, pair, chunk, span):
    y = fibre_conv(g, w, pair, aligned(chunk, span)).reshape(span // 8, 8, 256)
    z = jnp.concatenate([y[:, :, :128], y[:, :, 128:]], axis=1).reshape(span // 16, 2, 16, 128)
    z = jnp.concatenate([z[:, 0], z[:, 1]], axis=2)
    rows, q0 = aligned(pair, 16), chunk * (span // 16)
    dp[pl.ds(2 + q0, span // 16), rows, :] = (z * slope[pl.ds(q0, span // 16), rows, :]).astype(BF)


def do_grad_time(xtt, dp, acc, q0, count):
    lhs = [jnp.concatenate([xtt[q0 + b + j] for j in range(count)], axis=1) for b in range(5)]
    acc[...] += dot(jnp.concatenate(lhs, axis=0), dp[pl.ds(2 + q0, count)].reshape(count * 128, 256))


def do_grad_fibre(gt, h, acc, pair):
    lhs = gt[pl.ds(pair, 5)].reshape(1280, gt.shape[2])
    acc[...] += dot(lhs, jnp.concatenate([h[4 + 2 * pair], h[5 + 2 * pair]], axis=1))


def do_d_records(dp, w, g, out, q0):
    y = time_conv(dp, w, q0)
    for j in range(TILE):
        at = aligned(q0 + j, 16)
        out[:, at, :] = (g[4:20, at, :].astype(F32) + natural(y[128 * j : 128 * j + 128])).astype(BF)


def do_mixed(h, w, x, out, pair, at):
    y = fibre_conv(h, w, pair, at)
    out[2 * pair, at] = (x[2 * pair, at].astype(F32) + y[:, :128]).astype(BF)
    out[2 * pair + 1, at] = (x[2 * pair + 1, at].astype(F32) + y[:, 128:]).astype(BF)


def fold(acc, grads):
    def part(i, b, e, d):
        return acc[i, 256 * b + 128 * e : 256 * b + 128 * e + 128, 128 * d : 128 * d + 128]

    for k in range(9):
        if k % 2 == 0:
            low, high = k // 2, (8 - k) // 2
            grads[0, k] = part(0, low, 0, 0) + part(0, low, 1, 1)
            grads[1, k] = (part(1, high, 0, 0) + part(1, high, 1, 1)).T
        else:
            grads[0, k] = part(0, (k - 1) // 2, 1, 0) + part(0, (k + 1) // 2, 0, 1)
            grads[1, k] = (part(1, (9 - k) // 2, 0, 1) + part(1, (7 - k) // 2, 1, 0)).T


def kernel(factor, x_hbm, tw_hbm, fw_hbm, g_hbm, mixed, d_rec, gt_out, gf_out,
           x, g, h, xt, xtt, gt, dp, slope, mix, drec, wraw, big, acc, grads, other, parts, inbox, planes, gathered,
           lsem, gsend, grecv, hsend, hrecv, xsend, xrecv, dsend, drecv, asem, bsend, brecv, csend, crecv, esend, erecv,
           fsem):
    fi, ti, ri = lax.axis_index("fibre"), lax.axis_index("tm"), lax.axis_index("rep")
    nf, nt, nr = lax.axis_size("fibre"), lax.axis_size("tm"), lax.axis_size("rep")
    core = lax.rem(ti, 2)
    members = (nt // 2) * nr
    me = lax.div(ti, 2) * nr + ri
    rows = 128 // members
    used = 9 * rows

    def member(index):
        return {"tm": 2 * lax.div(index, nr) + core, "rep": lax.rem(index, nr)}

    def shifted(axis, index, count, step):
        return {axis: lax.rem(index + step + count, count)}

    partner = {"tm": ti + 1 - 2 * core}

    x_edges = [pltpu.make_async_copy(x_hbm.at[:, at, :], x.at[:, at, :], lsem.at[i])
               for i, at in enumerate((slice(0, 32), slice(480, 512)))]
    x_rest = pltpu.make_async_copy(x_hbm.at[:, 32:480, :], x.at[:, 32:480, :], lsem.at[2])
    w_time = pltpu.make_async_copy(tw_hbm, wraw.at[0], lsem.at[3])
    w_fibre = pltpu.make_async_copy(fw_hbm, wraw.at[1], lsem.at[4])
    g_load = pltpu.make_async_copy(g_hbm, g.at[4:20], lsem.at[5])
    for c in (*x_edges, w_time, x_rest, w_fibre, g_load):
        c.start()

    barrier = pltpu.get_barrier_semaphore()
    others = [shifted("fibre", fi, nf, d) for d in range(1, nf)]
    others += [shifted("tm", ti, nt, d) for d in (1, -1)]
    others += [member(lax.rem(me + d, members)) for d in range(1, members)]
    for d in others:
        pl.semaphore_signal(barrier, inc=1, device_id=d, device_id_type=MESH)
    pl.semaphore_wait(barrier, len(others))

    class Halo:
        def __init__(self, axis, index, count, pieces, send, recv):
            self.has = (index < count - 1, index > 0)
            self.copies = [
                [pltpu.make_async_remote_copy(
                    src_ref=src, dst_ref=dst, send_sem=send.at[side, i], recv_sem=recv.at[side, i],
                    device_id=shifted(axis, index, count, 1 - 2 * side), device_id_type=MESH)
                 for side, (src, dst) in enumerate(piece)]
                for i, piece in enumerate(pieces)]

        def start(self, i):
            for side in range(2):
                pl.when(self.has[side])(self.copies[i][side].start)

        def wait_recv(self, i):
            for side in range(2):
                pl.when(self.has[1 - side])(self.copies[i][side].wait_recv)

        def wait_send(self, i):
            for side in range(2):
                pl.when(self.has[side])(self.copies[i][side].wait_send)

    span = 512 // CHUNKS
    times = [slice(span * i, span * i + span) for i in range(CHUNKS)]
    g_halo = Halo("fibre", fi, nf, [
        ((g_hbm.at[12:16, at, :], g.at[0:4, at, :]), (g_hbm.at[0:4, at, :], g.at[20:24, at, :])) for at in times
    ], gsend, grecv)
    h_halo = Halo("fibre", fi, nf, [
        ((h.at[16:20, at, :], h.at[0:4, at, :]), (h.at[4:8, at, :], h.at[20:24, at, :])) for at in times
    ], hsend, hrecv)
    x_halo = Halo("tm", ti, nt, [((xt.at[32:34], xt.at[0:2]), (xt.at[2:4], xt.at[34:36]))], xsend, xrecv)
    d_halo = Halo("tm", ti, nt, [((dp.at[32:34], dp.at[0:2]), (dp.at[2:4], dp.at[34:36]))], dsend, drecv)
    for i in range(CHUNKS):
        g_halo.start(i)

    def build(q):
        v = to_time_pairs(x, q)
        xt[q + 2] = v
        xtt[q + 2] = v.T

    for c in x_edges:
        c.wait()
    for q in (0, 1, 30, 31):
        build(q)
    x_halo.start(0)

    for edge, at, time_at in ((0, slice(0, 4), slice(0, 2)), (1, slice(20, 24), slice(34, 36))):
        @pl.when((fi == 0) if edge == 0 else (fi == nf - 1))
        def _(at=at):
            g[at] = jnp.zeros((4, 512, 128), BF)
            h[at] = jnp.zeros((4, 512, 128), BF)

        @pl.when((ti == 0) if edge == 0 else (ti == nt - 1))
        def _(at=time_at):
            xt[at] = jnp.zeros((2, 128, 256), BF)
            dp[at] = jnp.zeros((2, 128, 256), BF)

    w_time.wait()
    pair_weights(big.at[0], lambda k: wraw[0, k])
    x_rest.wait()
    loop(2, 30, build)
    last = 32 // TILE - 1
    loop(1, last, lambda i: do_hidden(xt, big.at[0], h, slope, i * TILE))

    w_fibre.wait()
    pair_weights(big.at[1], lambda k: wraw[1, 8 - k].T)
    pair_weights(big.at[2], lambda k: wraw[1, k])
    pair_weights(big.at[3], lambda k: wraw[0, 8 - k].T)

    x_halo.wait_recv(0)
    for q in (0, 1, 34, 35):
        xtt[q] = xt[q].T
    do_hidden(xt, big.at[0], h, slope, last * TILE)
    do_hidden(xt, big.at[0], h, slope, 0)

    g_load.wait()

    def turn(p):
        for at in (slice(0, 128), slice(128, 256), slice(256, 384), slice(384, 512)):
            gt[p, :, at] = jnp.concatenate([g[2 * p, at], g[2 * p + 1, at]], axis=1).T

    acc[...] = jnp.zeros(acc.shape, F32)
    loop(2, 10, turn)
    loop(2, 6, lambda p: do_d_pre(g, big.at[1], slope, dp, p, 0, 512))
    loop(2, 6, lambda p: do_grad_fibre(gt, h, acc.at[1], p))
    loop(2, 6, lambda p: do_mixed(h, big.at[2], x, mix, p, slice(0, 512)))

    for i in range(CHUNKS):
        g_halo.wait_recv(i)
    for i in range(CHUNKS):
        h_halo.start(i)
    for p in (0, 1, 6, 7):
        do_d_pre(g, big.at[1], slope, dp, p, 0, 512)
    d_halo.start(0)
    loop(0, 8, lambda i: do_grad_time(xtt, dp, acc.at[0], 4 * i, 4))
    for p in (0, 1, 10, 11):
        turn(p)
    for p in (0, 1, 6, 7):
        do_grad_fibre(gt, h, acc.at[1], p)
    fold(acc, grads)

    swap = pltpu.make_async_remote_copy(
        src_ref=grads.at[1 - core], dst_ref=other, send_sem=asem.at[0], recv_sem=asem.at[1],
        device_id=partner, device_id_type=MESH)
    swap.start()
    loop(1, last, lambda i: do_d_records(dp, big.at[3], g, drec, i * TILE))
    swap.wait_recv()

    pad = jnp.zeros((parts.shape[1] - used, 128), F32) if parts.shape[1] > used else None

    def padded(v):
        return v if pad is None else jnp.concatenate([v, pad], axis=0)

    for s in range(members):
        at = slice(rows * s, rows * s + rows)
        parts[s] = padded((grads[core, :, at] + other[:, at]).reshape(used, 128)).astype(BF)
    mine = aligned(me, rows)
    own = (grads[core, :, mine] + other[:, mine]).reshape(used, 128)
    scatter = []
    for d in range(1, members):
        to = lax.rem(me + d, members)
        scatter.append(pltpu.make_async_remote_copy(
            src_ref=parts.at[to], dst_ref=inbox.at[d], send_sem=bsend.at[d], recv_sem=brecv.at[d],
            device_id=member(to), device_id_type=MESH))
    for c in scatter:
        c.start()

    d_halo.wait_recv(0)
    do_d_records(dp, big.at[3], g, drec, last * TILE)
    do_d_records(dp, big.at[3], g, drec, 0)
    out_d = pltpu.make_async_copy(drec, d_rec, lsem.at[6])
    out_d.start()

    for d, c in enumerate(scatter, 1):
        c.wait_recv()
        own = own + inbox[d].astype(F32)[:used]
    planes[fi] = own
    spread = []
    for d in range(1, nf):
        to = lax.rem(fi + d, nf)
        spread.append(pltpu.make_async_remote_copy(
            src_ref=planes.at[fi], dst_ref=planes.at[fi], send_sem=csend.at[d], recv_sem=crecv.at[d],
            device_id={"fibre": to}, device_id_type=MESH))
    for c in spread:
        c.start()

    for p in (0, 1, 6, 7):
        pass
    for d in range(1, nf):
        source = lax.rem(fi - d + nf, nf)
        pltpu.make_async_remote_copy(
            src_ref=planes.at[source], dst_ref=planes.at[source], send_sem=csend.at[d], recv_sem=crecv.at[d],
            device_id={"fibre": source}, device_id_type=MESH).wait_recv()
    total = planes[0]
    for i in range(1, nf):
        total = total + planes[i]
    gathered[core, me] = padded(total * factor).astype(BF)
    gather = []
    for d in range(1, members):
        gather.append(pltpu.make_async_remote_copy(
            src_ref=gathered.at[core, me], dst_ref=gathered.at[core, me], send_sem=esend.at[d], recv_sem=erecv.at[d],
            device_id=member(lax.rem(me + d, members)), device_id_type=MESH))
    for c in gather:
        c.start()

    for i in range(CHUNKS):
        h_halo.wait_recv(i)
        for p in (0, 1, 6, 7):
            do_mixed(h, big.at[2], x, mix, p, times[i])
    out_m = pltpu.make_async_copy(mix, mixed, lsem.at[7])
    out_m.start()

    for d in range(1, members):
        source = lax.rem(me - d + members, members)
        pltpu.make_async_remote_copy(
            src_ref=gathered.at[core, source], dst_ref=gathered.at[core, source], send_sem=esend.at[d],
            recv_sem=erecv.at[d], device_id=member(source), device_id_type=MESH).wait_recv()
    final = pltpu.make_async_remote_copy(
        src_ref=gathered.at[core], dst_ref=gathered.at[core], send_sem=fsem.at[0], recv_sem=fsem.at[1],
        device_id=partner, device_id_type=MESH)
    final.start()
    final.wait_send()
    pltpu.make_async_remote_copy(
        src_ref=gathered.at[1 - core], dst_ref=gathered.at[1 - core], send_sem=fsem.at[0], recv_sem=fsem.at[1],
        device_id=partner, device_id_type=MESH).wait_recv()
    for i, out in enumerate((gt_out, gf_out)):
        for s in range(members):
            out[:, rows * s : rows * s + rows] = gathered[i, s].astype(F32)[:used].reshape(9, rows, 128)

    swap.wait_send()
    for c in (*scatter, *spread, *gather):
        c.wait_send()
    for halo, count in ((g_halo, CHUNKS), (h_halo, CHUNKS), (x_halo, 1), (d_halo, 1)):
        for i in range(count):
            halo.wait_send(i)
    out_d.wait()
    out_m.wait()


def shards(factor, records, time_weight, fibre_weight, cotangent):
    nf, nt, nr = lax.axis_size("fibre"), lax.axis_size("tm"), lax.axis_size("rep")
    members = (nt // 2) * nr
    used = 9 * (128 // members)
    height = -(-used // 16) * 16
    dma = pltpu.SemaphoreType.DMA
    any_space, vmem = pl.BlockSpec(memory_space=pl.ANY), pl.BlockSpec(memory_space=pltpu.VMEM)
    field = jax.ShapeDtypeStruct((16, 512, 128), BF)
    grad = jax.ShapeDtypeStruct((9, 128, 128), F32)
    mixed, d_records, grad_time, grad_fibre = pl.pallas_call(
        functools.partial(kernel, factor),
        out_shape=(field, field, grad, grad),
        in_specs=[any_space] * 4,
        out_specs=(any_space, any_space, vmem, vmem),
        scratch_shapes=[
            pltpu.VMEM((16, 512, 128), BF),
            pltpu.VMEM((24, 512, 128), BF),
            pltpu.VMEM((24, 512, 128), BF),
            pltpu.VMEM((36, 128, 256), BF),
            pltpu.VMEM((36, 256, 128), BF),
            pltpu.VMEM((12, 256, 512), BF),
            pltpu.VMEM((36, 128, 256), BF),
            pltpu.VMEM((32, 128, 256), F32),
            pltpu.VMEM((16, 512, 128), BF),
            pltpu.VMEM((16, 512, 128), BF),
            pltpu.VMEM((2, 9, 128, 128), BF),
            pltpu.VMEM((4, 1280, 256), BF),
            pltpu.VMEM((2, 1280, 256), F32),
            pltpu.VMEM((2, 9, 128, 128), F32),
            pltpu.VMEM((9, 128, 128), F32),
            pltpu.VMEM((members, height, 128), BF),
            pltpu.VMEM((members, height, 128), BF),
            pltpu.VMEM((nf, used, 128), F32),
            pltpu.VMEM((2, members, height, 128), BF),
            dma((8,)),
            dma((2, CHUNKS)), dma((2, CHUNKS)), dma((2, CHUNKS)), dma((2, CHUNKS)),
            dma((2, 1)), dma((2, 1)), dma((2, 1)), dma((2, 1)),
            dma((2,)), dma((members,)), dma((members,)), dma((nf,)), dma((nf,)), dma((members,)), dma((members,)),
            dma((2,)),
        ],
        compiler_params=pltpu.CompilerParams(
            collective_id=0, has_side_effects=True, vmem_limit_bytes=56 << 20
        ),
        cost_estimate=pl.CostEstimate(flops=16 * 10**9, bytes_accessed=10**7, transcendentals=10**6),
        name="block",
    )(records[0], time_weight, fibre_weight, cotangent[0])
    return mixed[None], d_records[None], grad_time, grad_fibre


def solution(mesh):
    spec = P("rep", "fibre", "tm", None)
    total = 8 * 64 * 2048
    return jax.shard_map(
        functools.partial(shards, float(total) ** -0.5),
        mesh=mesh,
        in_specs=(spec, P(), P(), spec),
        out_specs=(spec, spec, P(), P()),
        check_vma=False,
    )
```

```python
import functools

import jax
import jax.numpy as jnp
from jax import lax
from jax.experimental import pallas as pl
from jax.experimental.pallas import tpu as pltpu
from jax.sharding import PartitionSpec as P

MESH = pl.DeviceIdType.MESH
BF, F32 = jnp.bfloat16, jnp.float32
TILE = 4
SPANS = (slice(0, 128), slice(128, 256), slice(256, 384), slice(384, 512))
CHUNKS = len(SPANS)
EDGES = (0, 1, 6, 7)
WIRE = BF


def dot(a, b):
    return jnp.dot(a, b, preferred_element_type=F32)


def loop(low, high, body):
    lax.fori_loop(low, high, lambda i, c: (body(i), c)[1], 0, unroll=high - low)


def aligned(index, size):
    return pl.ds(pl.multiple_of(index * size, size), size)


def pair_weights(dst, block):
    zero = jnp.zeros((128, 128), BF)
    for b in range(5):
        top, low = slice(256 * b, 256 * b + 128), slice(256 * b + 128, 256 * b + 256)
        dst[top, 0:128] = block(2 * b)
        dst[top, 128:256] = block(2 * b - 1) if b > 0 else zero
        dst[low, 0:128] = block(2 * b + 1) if b < 4 else zero
        dst[low, 128:256] = block(2 * b)


def to_time_pairs(src, q):
    v = src[:, aligned(q, 16), :].astype(F32)
    lo, hi = v[:, 0:8].reshape(128, 128), v[:, 8:16].reshape(128, 128)
    return jnp.concatenate([lo, hi], axis=1).astype(BF)


def natural(y):
    y = y.reshape(16, 8, 256)
    return jnp.concatenate([y[:, :, :128], y[:, :, 128:]], axis=1)


def time_conv(src, w, q0):
    lhs = [src[pl.ds(q0 + b, TILE)].reshape(TILE * 128, 256) for b in range(5)]
    return dot(jnp.concatenate(lhs, axis=1), w[...])


def do_hidden(xt, w, h, slope, q0):
    y = time_conv(xt, w, q0)
    s = 0.5 * jnp.tanh(0.5 * y) + 0.5
    hid = y * s
    slope[pl.ds(q0, TILE)] = (s + hid * (1.0 - s)).reshape(TILE, 128, 256)
    for j in range(TILE):
        h[4:20, aligned(q0 + j, 16), :] = natural(hid[128 * j : 128 * j + 128]).astype(BF)


def fibre_rows(src, items):
    return jnp.concatenate(
        [jnp.concatenate([src[2 * p + i, at] for i in range(10)], axis=1) for p, at in items], axis=0
    )


def split_rows(y, items):
    low = 0
    for p, at in items:
        size = at.stop - at.start
        yield p, at, size, y[low : low + size]
        low += size


def do_d_pre(g, w, slope, dp, items):
    for p, at, size, z in split_rows(dot(fibre_rows(g, items), w[...]), items):
        count, q0 = size // 16, at.start // 16
        z = z.reshape(size // 8, 8, 256)
        z = jnp.concatenate([z[:, :, :128], z[:, :, 128:]], axis=1).reshape(count, 2, 16, 128)
        z = jnp.concatenate([z[:, 0], z[:, 1]], axis=2)
        rows = aligned(p, 16)
        dp[2 + q0 : 2 + q0 + count, rows, :] = (z * slope[q0 : q0 + count, rows, :]).astype(BF)


def do_grad_fibre(gt, h, acc, items):
    lhs = [gt[pl.ds(p, 5), :, at].reshape(1280, at.stop - at.start) for p, at in items]
    rhs = [jnp.concatenate([h[4 + 2 * p, at], h[5 + 2 * p, at]], axis=1) for p, at in items]
    acc[...] += dot(jnp.concatenate(lhs, axis=1), jnp.concatenate(rhs, axis=0))


def do_mixed(h, w, x, out, items):
    for p, at, size, z in split_rows(dot(fibre_rows(h, items), w[...]), items):
        out[2 * p, at] = (x[2 * p, at].astype(F32) + z[:, :128]).astype(BF)
        out[2 * p + 1, at] = (x[2 * p + 1, at].astype(F32) + z[:, 128:]).astype(BF)


def do_grad_time(xtt, dp, acc, q0, count):
    lhs = [jnp.concatenate([xtt[q0 + b + j] for j in range(count)], axis=1) for b in range(5)]
    acc[...] += dot(jnp.concatenate(lhs, axis=0), dp[pl.ds(2 + q0, count)].reshape(count * 128, 256))


def do_d_records(dp, w, g, out, q0):
    y = time_conv(dp, w, q0)
    for j in range(TILE):
        at = aligned(q0 + j, 16)
        out[:, at, :] = (g[4:20, at, :].astype(F32) + natural(y[128 * j : 128 * j + 128])).astype(BF)


def fold(acc, grads):
    def part(i, b, e, d):
        return acc[i, 256 * b + 128 * e : 256 * b + 128 * e + 128, 128 * d : 128 * d + 128]

    for k in range(9):
        if k % 2 == 0:
            low, high = k // 2, (8 - k) // 2
            grads[0, k] = part(0, low, 0, 0) + part(0, low, 1, 1)
            grads[1, k] = (part(1, high, 0, 0) + part(1, high, 1, 1)).T
        else:
            grads[0, k] = part(0, (k - 1) // 2, 1, 0) + part(0, (k + 1) // 2, 0, 1)
            grads[1, k] = (part(1, (9 - k) // 2, 0, 1) + part(1, (7 - k) // 2, 1, 0)).T


def kernel(factor, x_hbm, tw_hbm, fw_hbm, g_hbm, mix, drec, gathered,
           x, g, h, xt, xtt, gt, dp, slope, wraw, big, acc, grads, other, parts, inbox, planes,
           lsem, gsend, grecv, hsend, hrecv, xsend, xrecv, dsend, drecv, asem, bsend, brecv, csend, crecv, esend, erecv,
           fsend, frecv):
    fi, ti, ri = lax.axis_index("fibre"), lax.axis_index("tm"), lax.axis_index("rep")
    nf, nt, nr = lax.axis_size("fibre"), lax.axis_size("tm"), lax.axis_size("rep")
    core = lax.rem(ti, 2)
    members = (nt // 2) * nr
    me = lax.div(ti, 2) * nr + ri
    rows = 128 // members
    used = 9 * rows

    def member(index):
        return {"tm": 2 * lax.div(index, nr) + core, "rep": lax.rem(index, nr)}

    def shifted(axis, index, count, step):
        return {axis: lax.rem(index + step + count, count)}

    partner = {"tm": ti + 1 - 2 * core}

    x_edges = [pltpu.make_async_copy(x_hbm.at[:, at, :], x.at[:, at, :], lsem.at[i])
               for i, at in enumerate((slice(0, 32), slice(480, 512)))]
    x_rest = pltpu.make_async_copy(x_hbm.at[:, 32:480, :], x.at[:, 32:480, :], lsem.at[2])
    w_time = pltpu.make_async_copy(tw_hbm, wraw.at[0], lsem.at[3])
    w_fibre = pltpu.make_async_copy(fw_hbm, wraw.at[1], lsem.at[4])
    g_load = pltpu.make_async_copy(g_hbm, g.at[4:20], lsem.at[5])
    for c in (*x_edges, w_time, x_rest, w_fibre, g_load):
        c.start()

    barrier = pltpu.get_barrier_semaphore()
    others = [shifted("fibre", fi, nf, d) for d in range(1, nf)]
    others += [shifted("tm", ti, nt, d) for d in (1, -1)]
    others += [member(lax.rem(me + d, members)) for d in range(1, members)]
    for d in others:
        pl.semaphore_signal(barrier, inc=1, device_id=d, device_id_type=MESH)
    class Halo:
        def __init__(self, axis, index, count, pieces, send, recv):
            self.has = (index < count - 1, index > 0)
            self.copies = [
                [pltpu.make_async_remote_copy(
                    src_ref=src, dst_ref=dst, send_sem=send.at[side, i], recv_sem=recv.at[side, i],
                    device_id=shifted(axis, index, count, 1 - 2 * side), device_id_type=MESH)
                 for side, (src, dst) in enumerate(piece)]
                for i, piece in enumerate(pieces)]

        def start(self, i):
            for side in range(2):
                pl.when(self.has[side])(self.copies[i][side].start)

        def wait_recv(self, i):
            for side in range(2):
                pl.when(self.has[1 - side])(self.copies[i][side].wait_recv)

        def wait_send(self, i):
            for side in range(2):
                pl.when(self.has[side])(self.copies[i][side].wait_send)

    g_halo = Halo("fibre", fi, nf, [
        ((g_hbm.at[12:16, at, :], g.at[0:4, at, :]), (g_hbm.at[0:4, at, :], g.at[20:24, at, :])) for at in SPANS
    ], gsend, grecv)
    h_halo = Halo("fibre", fi, nf, [
        ((h.at[16:20, at, :], h.at[0:4, at, :]), (h.at[4:8, at, :], h.at[20:24, at, :])) for at in SPANS
    ], hsend, hrecv)
    x_halo = Halo("tm", ti, nt, [((xt.at[32:34], xt.at[0:2]), (xt.at[2:4], xt.at[34:36]))], xsend, xrecv)
    d_halo = Halo("tm", ti, nt, [((dp.at[32:34], dp.at[0:2]), (dp.at[2:4], dp.at[34:36]))], dsend, drecv)
    def build(q):
        v = to_time_pairs(x, q)
        xt[q + 2] = v
        xtt[q + 2] = v.T

    for c in x_edges:
        c.wait()
    for q in (0, 1, 30, 31):
        build(q)
    pl.semaphore_wait(barrier, len(others))
    x_halo.start(0)
    for i in range(CHUNKS):
        g_halo.start(i)

    for edge, at, time_at in ((0, slice(0, 4), slice(0, 2)), (1, slice(20, 24), slice(34, 36))):
        @pl.when((fi == 0) if edge == 0 else (fi == nf - 1))
        def _(at=at):
            g[at] = jnp.zeros((4, 512, 128), BF)
            h[at] = jnp.zeros((4, 512, 128), BF)

        @pl.when((ti == 0) if edge == 0 else (ti == nt - 1))
        def _(at=time_at):
            xt[at] = jnp.zeros((2, 128, 256), BF)
            dp[at] = jnp.zeros((2, 128, 256), BF)

    w_time.wait()
    pair_weights(big.at[0], lambda k: wraw[0, k])
    x_rest.wait()
    loop(2, 30, build)
    last = 32 // TILE - 1
    loop(1, last, lambda i: do_hidden(xt, big.at[0], h, slope, i * TILE))

    w_fibre.wait()
    pair_weights(big.at[1], lambda k: wraw[1, 8 - k].T)
    pair_weights(big.at[2], lambda k: wraw[1, k])
    pair_weights(big.at[3], lambda k: wraw[0, 8 - k].T)

    g_load.wait()

    def turn(p, spans):
        for at in spans:
            gt[p, :, at] = jnp.concatenate([g[2 * p, at], g[2 * p + 1, at]], axis=1).T

    acc[...] = jnp.zeros(acc.shape, F32)
    quarters = [slice(128 * i, 128 * i + 128) for i in range(4)]
    loop(2, 10, lambda p: turn(p, quarters))
    inner, outer = (slice(128, 384),), (quarters[0], quarters[3])
    loop(2, 6, lambda p: do_d_pre(g, big.at[1], slope, dp, [(p, at) for at in inner]))
    loop(2, 6, lambda p: do_grad_fibre(gt, h, acc.at[1], [(p, at) for at in inner]))

    x_halo.wait_recv(0)
    for q in (0, 1, 34, 35):
        xtt[q] = xt[q].T
    do_hidden(xt, big.at[0], h, slope, last * TILE)
    do_hidden(xt, big.at[0], h, slope, 0)
    loop(2, 6, lambda p: do_d_pre(g, big.at[1], slope, dp, [(p, at) for at in outer]))
    loop(2, 6, lambda p: do_grad_fibre(gt, h, acc.at[1], [(p, at) for at in outer]))

    for i, at in enumerate(SPANS):
        g_halo.wait_recv(i)
        if i == CHUNKS - 1:
            for j in range(CHUNKS):
                h_halo.start(j)
        items = [(p, at) for p in EDGES]
        do_d_pre(g, big.at[1], slope, dp, items)
        if i == CHUNKS - 1:
            d_halo.start(0)
        for p in (0, 1, 10, 11):
            turn(p, [at])
        do_grad_fibre(gt, h, acc.at[1], items)
        loop(at.start // 64, at.stop // 64, lambda q: do_grad_time(xtt, dp, acc.at[0], 4 * q, 4))
    fold(acc, grads)

    swap = pltpu.make_async_remote_copy(
        src_ref=grads.at[1 - core], dst_ref=other, send_sem=asem.at[0], recv_sem=asem.at[1],
        device_id=partner, device_id_type=MESH)
    swap.start()
    loop(2, 6, lambda p: do_mixed(h, big.at[2], x, mix, [(p, slice(0, 512))]))
    swap.wait_recv()

    pad = jnp.zeros((parts.shape[1] - used, 128), F32) if parts.shape[1] > used else None

    def padded(v):
        return v if pad is None else jnp.concatenate([v, pad], axis=0)

    for s in range(members):
        at = slice(rows * s, rows * s + rows)
        parts[s] = padded((grads[core, :, at] + other[:, at]).reshape(used, 128)).astype(WIRE)
    mine = aligned(me, rows)
    own = (grads[core, :, mine] + other[:, mine]).reshape(used, 128)
    scatter = []
    for d in range(1, members):
        to = lax.rem(me + d, members)
        scatter.append(pltpu.make_async_remote_copy(
            src_ref=parts.at[to], dst_ref=inbox.at[d], send_sem=bsend.at[d], recv_sem=brecv.at[d],
            device_id=member(to), device_id_type=MESH))
    for c in scatter:
        c.start()

    loop(1, last, lambda i: do_d_records(dp, big.at[3], g, drec, i * TILE))
    for d, c in enumerate(scatter, 1):
        c.wait_recv()
        own = own + inbox[d].astype(F32)[:used]
    planes[fi] = own
    spread = []
    for d in range(1, nf):
        to = lax.rem(fi + d, nf)
        spread.append(pltpu.make_async_remote_copy(
            src_ref=planes.at[fi], dst_ref=planes.at[fi], send_sem=csend.at[d], recv_sem=crecv.at[d],
            device_id={"fibre": to}, device_id_type=MESH))
    for c in spread:
        c.start()

    d_halo.wait_recv(0)
    do_d_records(dp, big.at[3], g, drec, last * TILE)
    do_d_records(dp, big.at[3], g, drec, 0)
    for d in range(1, nf):
        source = lax.rem(fi - d + nf, nf)
        pltpu.make_async_remote_copy(
            src_ref=planes.at[source], dst_ref=planes.at[source], send_sem=csend.at[d], recv_sem=crecv.at[d],
            device_id={"fibre": source}, device_id_type=MESH).wait_recv()
    total = planes[0]
    for i in range(1, nf):
        total = total + planes[i]
    gathered[core, me] = padded(total * factor).astype(BF)
    gather = []
    for d in range(1, members):
        gather.append(pltpu.make_async_remote_copy(
            src_ref=gathered.at[core, me], dst_ref=gathered.at[core, me], send_sem=esend.at[d], recv_sem=erecv.at[d],
            device_id=member(lax.rem(me + d, members)), device_id_type=MESH))
    for c in gather:
        c.start()

    def forward(which, part, d):
        return pltpu.make_async_remote_copy(
            src_ref=gathered.at[which, part], dst_ref=gathered.at[which, part], send_sem=fsend.at[d],
            recv_sem=frecv.at[d], device_id=partner, device_id_type=MESH)

    passed = [forward(core, me, 0)]
    passed[0].start()
    for i in range(CHUNKS):
        h_halo.wait_recv(i)
        do_mixed(h, big.at[2], x, mix, [(p, SPANS[i]) for p in EDGES])

    for d in range(1, members):
        source = lax.rem(me - d + members, members)
        pltpu.make_async_remote_copy(
            src_ref=gathered.at[core, source], dst_ref=gathered.at[core, source], send_sem=esend.at[d],
            recv_sem=erecv.at[d], device_id=member(source), device_id_type=MESH).wait_recv()
        passed.append(forward(core, source, d))
        passed[-1].start()
    for d in range(members):
        forward(1 - core, lax.rem(me - d + members, members), d).wait_recv()

    swap.wait_send()
    for c in (*scatter, *spread, *gather, *passed):
        c.wait_send()
    for halo, count in ((g_halo, CHUNKS), (h_halo, CHUNKS), (x_halo, 1), (d_halo, 1)):
        for i in range(count):
            halo.wait_send(i)


def shards(factor, records, time_weight, fibre_weight, cotangent):
    nf, nt, nr = lax.axis_size("fibre"), lax.axis_size("tm"), lax.axis_size("rep")
    members = (nt // 2) * nr
    used = 9 * (128 // members)
    height = -(-used // 16) * 16
    dma = pltpu.SemaphoreType.DMA
    any_space = pl.BlockSpec(memory_space=pl.ANY)
    mix, drec, gathered = pl.pallas_call(
        functools.partial(kernel, factor),
        out_shape=(
            pltpu.VMEM((16, 512, 128), BF), pltpu.VMEM((16, 512, 128), BF), pltpu.VMEM((2, members, height, 128), BF)
        ),
        in_specs=[pl.BlockSpec(memory_space=pltpu.HBM)] * 4,
        out_specs=(pl.BlockSpec(memory_space=pltpu.VMEM),) * 3,
        scratch_shapes=[
            pltpu.VMEM((16, 512, 128), BF),
            pltpu.VMEM((24, 512, 128), BF),
            pltpu.VMEM((24, 512, 128), BF),
            pltpu.VMEM((36, 128, 256), BF),
            pltpu.VMEM((36, 256, 128), BF),
            pltpu.VMEM((12, 256, 512), BF),
            pltpu.VMEM((36, 128, 256), BF),
            pltpu.VMEM((32, 128, 256), F32),
            pltpu.VMEM((2, 9, 128, 128), BF),
            pltpu.VMEM((4, 1280, 256), BF),
            pltpu.VMEM((2, 1280, 256), F32),
            pltpu.VMEM((2, 9, 128, 128), F32),
            pltpu.VMEM((9, 128, 128), F32),
            pltpu.VMEM((members, height, 128), WIRE),
            pltpu.VMEM((members, height, 128), WIRE),
            pltpu.VMEM((nf, used, 128), F32),
            dma((8,)),
            dma((2, CHUNKS)), dma((2, CHUNKS)), dma((2, CHUNKS)), dma((2, CHUNKS)),
            dma((2, 1)), dma((2, 1)), dma((2, 1)), dma((2, 1)),
            dma((2,)), dma((members,)), dma((members,)), dma((nf,)), dma((nf,)), dma((members,)), dma((members,)),
            dma((members,)), dma((members,)),
        ],
        compiler_params=pltpu.CompilerParams(
            collective_id=0, has_side_effects=True, vmem_limit_bytes=48 << 20
        ),
        cost_estimate=pl.CostEstimate(flops=16 * 10**9, bytes_accessed=10**7, transcendentals=10**6),
        name="block",
    )(*(pltpu.with_memory_space_constraint(a, pltpu.HBM) for a in (records[0], time_weight, fibre_weight, cotangent[0])))

    def store(mix, drec, gathered, mixed, d_records, grad_time, grad_fibre, staged, sem):
        copies = [pltpu.make_async_copy(mix, mixed, sem.at[0]), pltpu.make_async_copy(drec, d_records, sem.at[1])]
        for c in copies:
            c.start()
        rows = 128 // members
        for i, out in enumerate((grad_time, grad_fibre)):
            for s in range(members):
                staged[i, :, rows * s : rows * s + rows] = gathered[i, s].astype(F32)[:used].reshape(9, rows, 128)
            copies.append(pltpu.make_async_copy(staged.at[i], out, sem.at[2 + i]))
            copies[-1].start()
        for c in copies:
            c.wait()

    field = jax.ShapeDtypeStruct((16, 512, 128), BF)
    grad = jax.ShapeDtypeStruct((9, 128, 128), F32)
    mixed, d_records, grad_time, grad_fibre = pl.pallas_call(
        store,
        out_shape=(field, field, grad, grad),
        in_specs=[any_space, any_space, pl.BlockSpec(memory_space=pltpu.VMEM)],
        out_specs=(any_space,) * 4,
        scratch_shapes=[pltpu.VMEM((2, 9, 128, 128), F32), dma((4,))],
        compiler_params=pltpu.CompilerParams(vmem_limit_bytes=8 << 20),
        cost_estimate=pl.CostEstimate(flops=0, bytes_accessed=10**7, transcendentals=0),
        name="store",
    )(mix, drec, gathered)
    return mixed[None], d_records[None], grad_time, grad_fibre


def solution(mesh):
    spec = P("rep", "fibre", "tm", None)
    total = 8 * 64 * 2048
    return jax.shard_map(
        functools.partial(shards, float(total) ** -0.5),
        mesh=mesh,
        in_specs=(spec, P(), P(), spec),
        out_specs=(spec, spec, P(), P()),
        check_vma=False,
    )
```

```python
import functools

import jax
import jax.numpy as jnp
from jax import lax
from jax.experimental import pallas as pl
from jax.experimental.pallas import tpu as pltpu
from jax.sharding import PartitionSpec as P

MESH = pl.DeviceIdType.MESH
BF, F32 = jnp.bfloat16, jnp.float32
TILE = 4
SPANS = (slice(0, 256), slice(256, 512))
CHUNKS = len(SPANS)
EDGES = (0, 1, 6, 7)
WIRE = BF


def dot(a, b):
    return jnp.dot(a, b, preferred_element_type=F32)


def loop(low, high, body):
    lax.fori_loop(low, high, lambda i, c: (body(i), c)[1], 0, unroll=high - low)


def aligned(index, size):
    return pl.ds(pl.multiple_of(index * size, size), size)


def pair_weights(dst, block):
    zero = jnp.zeros((128, 128), BF)
    for b in range(5):
        top, low = slice(256 * b, 256 * b + 128), slice(256 * b + 128, 256 * b + 256)
        dst[top, 0:128] = block(2 * b)
        dst[top, 128:256] = block(2 * b - 1) if b > 0 else zero
        dst[low, 0:128] = block(2 * b + 1) if b < 4 else zero
        dst[low, 128:256] = block(2 * b)


def to_time_pairs(src, q):
    v = src[:, aligned(q, 16), :].astype(F32)
    lo, hi = v[:, 0:8].reshape(128, 128), v[:, 8:16].reshape(128, 128)
    return jnp.concatenate([lo, hi], axis=1).astype(BF)


def natural(y):
    y = y.reshape(16, 8, 256)
    return jnp.concatenate([y[:, :, :128], y[:, :, 128:]], axis=1)


def time_conv(src, w, q0):
    lhs = [src[pl.ds(q0 + b, TILE)].reshape(TILE * 128, 256) for b in range(5)]
    return dot(jnp.concatenate(lhs, axis=1), w[...])


def do_hidden(xt, w, h, slope, q0):
    y = time_conv(xt, w, q0)
    s = 0.5 * jnp.tanh(0.5 * y) + 0.5
    hid = y * s
    slope[pl.ds(q0, TILE)] = (s + hid * (1.0 - s)).reshape(TILE, 128, 256)
    for j in range(TILE):
        h[4:20, aligned(q0 + j, 16), :] = natural(hid[128 * j : 128 * j + 128]).astype(BF)


def fibre_rows(src, items):
    return jnp.concatenate(
        [jnp.concatenate([src[2 * p + i, at] for i in range(10)], axis=1) for p, at in items], axis=0
    )


def split_rows(y, items):
    low = 0
    for p, at in items:
        size = at.stop - at.start
        yield p, at, size, y[low : low + size]
        low += size


def do_d_pre(g, w, slope, dp, items):
    for p, at, size, z in split_rows(dot(fibre_rows(g, items), w[...]), items):
        count, q0 = size // 16, at.start // 16
        z = z.reshape(size // 8, 8, 256)
        z = jnp.concatenate([z[:, :, :128], z[:, :, 128:]], axis=1).reshape(count, 2, 16, 128)
        z = jnp.concatenate([z[:, 0], z[:, 1]], axis=2)
        rows = aligned(p, 16)
        dp[2 + q0 : 2 + q0 + count, rows, :] = (z * slope[q0 : q0 + count, rows, :]).astype(BF)


def do_grad_fibre(gt, h, acc, items):
    lhs = [gt[pl.ds(p, 5), :, at].reshape(1280, at.stop - at.start) for p, at in items]
    rhs = [jnp.concatenate([h[4 + 2 * p, at], h[5 + 2 * p, at]], axis=1) for p, at in items]
    acc[...] += dot(jnp.concatenate(lhs, axis=1), jnp.concatenate(rhs, axis=0))


def do_mixed(h, w, x, out, items):
    for p, at, size, z in split_rows(dot(fibre_rows(h, items), w[...]), items):
        out[2 * p, at] = (x[2 * p, at].astype(F32) + z[:, :128]).astype(BF)
        out[2 * p + 1, at] = (x[2 * p + 1, at].astype(F32) + z[:, 128:]).astype(BF)


def do_grad_time(xtt, dp, acc, q0, count):
    lhs = [jnp.concatenate([xtt[q0 + b + j] for j in range(count)], axis=1) for b in range(5)]
    acc[...] += dot(jnp.concatenate(lhs, axis=0), dp[pl.ds(2 + q0, count)].reshape(count * 128, 256))


def do_d_records(dp, w, g, out, q0):
    y = time_conv(dp, w, q0)
    for j in range(TILE):
        at = aligned(q0 + j, 16)
        out[:, at, :] = (g[4:20, at, :].astype(F32) + natural(y[128 * j : 128 * j + 128])).astype(BF)


def fold(acc, grads):
    def part(i, b, e, d):
        return acc[i, 256 * b + 128 * e : 256 * b + 128 * e + 128, 128 * d : 128 * d + 128]

    for k in range(9):
        if k % 2 == 0:
            low, high = k // 2, (8 - k) // 2
            grads[0, k] = part(0, low, 0, 0) + part(0, low, 1, 1)
            grads[1, k] = (part(1, high, 0, 0) + part(1, high, 1, 1)).T
        else:
            grads[0, k] = part(0, (k - 1) // 2, 1, 0) + part(0, (k + 1) // 2, 0, 1)
            grads[1, k] = (part(1, (9 - k) // 2, 0, 1) + part(1, (7 - k) // 2, 1, 0)).T


def kernel(factor, x_hbm, tw_hbm, fw_hbm, g_hbm, mix, drec, gathered,
           x, g, h, xt, xtt, gt, dp, slope, wraw, big, acc, grads, other, parts, inbox, planes,
           lsem, gsend, grecv, hsend, hrecv, xsend, xrecv, dsend, drecv, asem, bsend, brecv, csend, crecv, esend, erecv,
           fsem):
    fi, ti, ri = lax.axis_index("fibre"), lax.axis_index("tm"), lax.axis_index("rep")
    nf, nt, nr = lax.axis_size("fibre"), lax.axis_size("tm"), lax.axis_size("rep")
    core = lax.rem(ti, 2)
    members = (nt // 2) * nr
    me = lax.div(ti, 2) * nr + ri
    rows = 128 // members
    used = 9 * rows

    offsets = sorted(range(1, members), key=lambda d: -sum(min(i, 4 - i) for i in (d // 4, d % 4)))

    def moved(d, sign):
        return 4 * lax.rem(me // 4 + sign * (d // 4) + members, members // 4) + lax.rem(me % 4 + sign * (d % 4) + 4, 4)

    def member(index):
        return {"tm": 2 * lax.div(index, nr) + core, "rep": lax.rem(index, nr)}

    def shifted(axis, index, count, step):
        return {axis: lax.rem(index + step + count, count)}

    partner = {"tm": ti + 1 - 2 * core}

    barrier = pltpu.get_barrier_semaphore()
    others = [shifted("fibre", fi, nf, d) for d in range(1, nf)]
    others += [shifted("tm", ti, nt, d) for d in (1, -1)]
    others = [member(moved(d, 1)) for d in offsets] + others
    for d in others:
        pl.semaphore_signal(barrier, inc=1, device_id=d, device_id_type=MESH)

    x_edges = [pltpu.make_async_copy(x_hbm.at[:, at, :], x.at[:, at, :], lsem.at[i])
               for i, at in enumerate((slice(0, 32), slice(480, 512)))]
    x_rest = pltpu.make_async_copy(x_hbm.at[:, 32:480, :], x.at[:, 32:480, :], lsem.at[2])
    w_time = pltpu.make_async_copy(tw_hbm, wraw.at[0], lsem.at[3])
    w_fibre = pltpu.make_async_copy(fw_hbm, wraw.at[1], lsem.at[4])
    g_load = pltpu.make_async_copy(g_hbm, g.at[4:20], lsem.at[5])
    for c in (*x_edges, w_time, x_rest, w_fibre, g_load):
        c.start()

    class Halo:
        def __init__(self, axis, index, count, pieces, send, recv):
            self.has = (index < count - 1, index > 0)
            self.copies = [
                [pltpu.make_async_remote_copy(
                    src_ref=src, dst_ref=dst, send_sem=send.at[side, i], recv_sem=recv.at[side, i],
                    device_id=shifted(axis, index, count, 1 - 2 * side), device_id_type=MESH)
                 for side, (src, dst) in enumerate(piece)]
                for i, piece in enumerate(pieces)]

        def start(self, i):
            for side in range(2):
                pl.when(self.has[side])(self.copies[i][side].start)

        def wait_recv(self, i):
            for side in range(2):
                pl.when(self.has[1 - side])(self.copies[i][side].wait_recv)

        def wait_send(self, i):
            for side in range(2):
                pl.when(self.has[side])(self.copies[i][side].wait_send)

    g_halo = Halo("fibre", fi, nf, [
        ((g_hbm.at[12:16, at, :], g.at[0:4, at, :]), (g_hbm.at[0:4, at, :], g.at[20:24, at, :])) for at in SPANS
    ], gsend, grecv)
    h_halo = Halo("fibre", fi, nf, [
        ((h.at[16:20, at, :], h.at[0:4, at, :]), (h.at[4:8, at, :], h.at[20:24, at, :])) for at in SPANS
    ], hsend, hrecv)
    x_halo = Halo("tm", ti, nt, [((xt.at[32:34], xt.at[0:2]), (xt.at[2:4], xt.at[34:36]))], xsend, xrecv)
    d_halo = Halo("tm", ti, nt, [((dp.at[32:34], dp.at[0:2]), (dp.at[2:4], dp.at[34:36]))], dsend, drecv)
    def build(q):
        v = to_time_pairs(x, q)
        xt[q + 2] = v
        xtt[q + 2] = v.T

    pl.semaphore_wait(barrier, len(others))
    for i in range(CHUNKS):
        g_halo.start(i)
    for c in x_edges:
        c.wait()
    for q in (0, 1, 30, 31):
        build(q)
    x_halo.start(0)

    for edge, at, time_at in ((0, slice(0, 4), slice(0, 2)), (1, slice(20, 24), slice(34, 36))):
        @pl.when((fi == 0) if edge == 0 else (fi == nf - 1))
        def _(at=at):
            g[at] = jnp.zeros((4, 512, 128), BF)
            h[at] = jnp.zeros((4, 512, 128), BF)

        @pl.when((ti == 0) if edge == 0 else (ti == nt - 1))
        def _(at=time_at):
            xt[at] = jnp.zeros((2, 128, 256), BF)
            dp[at] = jnp.zeros((2, 128, 256), BF)

    w_time.wait()
    pair_weights(big.at[0], lambda k: wraw[0, k])
    x_rest.wait()
    loop(2, 30, build)
    last = 32 // TILE - 1
    loop(1, last, lambda i: do_hidden(xt, big.at[0], h, slope, i * TILE))

    w_fibre.wait()
    pair_weights(big.at[1], lambda k: wraw[1, 8 - k].T)
    pair_weights(big.at[2], lambda k: wraw[1, k])
    pair_weights(big.at[3], lambda k: wraw[0, 8 - k].T)

    g_load.wait()

    def turn(p, spans):
        for at in spans:
            gt[p, :, at] = jnp.concatenate([g[2 * p, at], g[2 * p + 1, at]], axis=1).T

    acc[...] = jnp.zeros(acc.shape, F32)
    quarters = [slice(128 * i, 128 * i + 128) for i in range(4)]
    loop(2, 10, lambda p: turn(p, quarters))
    inner, outer = (slice(128, 384),), (quarters[0], quarters[3])
    loop(2, 6, lambda p: do_d_pre(g, big.at[1], slope, dp, [(p, at) for at in inner]))
    loop(2, 6, lambda p: do_grad_fibre(gt, h, acc.at[1], [(p, at) for at in inner]))

    x_halo.wait_recv(0)
    for q in (0, 1, 34, 35):
        xtt[q] = xt[q].T
    do_hidden(xt, big.at[0], h, slope, last * TILE)
    do_hidden(xt, big.at[0], h, slope, 0)
    loop(2, 6, lambda p: do_d_pre(g, big.at[1], slope, dp, [(p, at) for at in outer]))
    loop(2, 6, lambda p: do_grad_fibre(gt, h, acc.at[1], [(p, at) for at in outer]))

    for i, at in enumerate(SPANS):
        g_halo.wait_recv(i)
        if i == CHUNKS - 1:
            for j in range(CHUNKS):
                h_halo.start(j)
        items = [(p, at) for p in EDGES]
        do_d_pre(g, big.at[1], slope, dp, items)
        if i == CHUNKS - 1:
            d_halo.start(0)
        for p in (0, 1, 10, 11):
            turn(p, [at])
        do_grad_fibre(gt, h, acc.at[1], items)
        loop(at.start // 64, at.stop // 64, lambda q: do_grad_time(xtt, dp, acc.at[0], 4 * q, 4))
    fold(acc, grads)

    swap = pltpu.make_async_remote_copy(
        src_ref=grads.at[1 - core], dst_ref=other, send_sem=asem.at[0], recv_sem=asem.at[1],
        device_id=partner, device_id_type=MESH)
    swap.start()
    loop(2, 6, lambda p: do_mixed(h, big.at[2], x, mix, [(p, slice(0, 512))]))
    swap.wait_recv()

    pad = jnp.zeros((parts.shape[1] - used, 128), F32) if parts.shape[1] > used else None

    def padded(v):
        return v if pad is None else jnp.concatenate([v, pad], axis=0)

    for s in range(members):
        at = slice(rows * s, rows * s + rows)
        parts[s] = padded((grads[core, :, at] + other[:, at]).reshape(used, 128)).astype(WIRE)
    mine = aligned(me, rows)
    own = (grads[core, :, mine] + other[:, mine]).reshape(used, 128)
    scatter = []
    for d in offsets:
        to = moved(d, 1)
        scatter.append(pltpu.make_async_remote_copy(
            src_ref=parts.at[to], dst_ref=inbox.at[d], send_sem=bsend.at[d], recv_sem=brecv.at[d],
            device_id=member(to), device_id_type=MESH))
    for c in scatter:
        c.start()

    loop(1, last, lambda i: do_d_records(dp, big.at[3], g, drec, i * TILE))
    for d, c in zip(offsets, scatter):
        c.wait_recv()
        own = own + inbox[d].astype(F32)[:used]
    planes[fi] = own
    spread = []
    for d in range(1, nf):
        to = lax.rem(fi + d, nf)
        spread.append(pltpu.make_async_remote_copy(
            src_ref=planes.at[fi], dst_ref=planes.at[fi], send_sem=csend.at[d], recv_sem=crecv.at[d],
            device_id={"fibre": to}, device_id_type=MESH))
    for c in spread:
        c.start()

    d_halo.wait_recv(0)
    do_d_records(dp, big.at[3], g, drec, last * TILE)
    do_d_records(dp, big.at[3], g, drec, 0)
    for d in range(1, nf):
        source = lax.rem(fi - d + nf, nf)
        pltpu.make_async_remote_copy(
            src_ref=planes.at[source], dst_ref=planes.at[source], send_sem=csend.at[d], recv_sem=crecv.at[d],
            device_id={"fibre": source}, device_id_type=MESH).wait_recv()
    total = planes[0]
    for i in range(1, nf):
        total = total + planes[i]
    gathered[core, me] = padded(total * factor).astype(BF)
    gather = []
    for d in offsets:
        gather.append(pltpu.make_async_remote_copy(
            src_ref=gathered.at[core, me], dst_ref=gathered.at[core, me], send_sem=esend.at[d], recv_sem=erecv.at[d],
            device_id=member(moved(d, 1)), device_id_type=MESH))
    for c in gather:
        c.start()

    for i in range(CHUNKS):
        h_halo.wait_recv(i)
        do_mixed(h, big.at[2], x, mix, [(p, SPANS[i]) for p in EDGES])

    for d in offsets:
        source = moved(d, -1)
        pltpu.make_async_remote_copy(
            src_ref=gathered.at[core, source], dst_ref=gathered.at[core, source], send_sem=esend.at[d],
            recv_sem=erecv.at[d], device_id=member(source), device_id_type=MESH).wait_recv()

    def forward(which):
        return pltpu.make_async_remote_copy(
            src_ref=gathered.at[which], dst_ref=gathered.at[which], send_sem=fsem.at[0],
            recv_sem=fsem.at[1], device_id=partner, device_id_type=MESH)

    forward(core).start()
    forward(1 - core).wait_recv()

    forward(core).wait_send()
    swap.wait_send()
    for c in (*scatter, *spread, *gather):
        c.wait_send()
    for halo, count in ((g_halo, CHUNKS), (h_halo, CHUNKS), (x_halo, 1), (d_halo, 1)):
        for i in range(count):
            halo.wait_send(i)


def shards(factor, records, time_weight, fibre_weight, cotangent):
    nf, nt, nr = lax.axis_size("fibre"), lax.axis_size("tm"), lax.axis_size("rep")
    members = (nt // 2) * nr
    used = 9 * (128 // members)
    height = -(-used // 16) * 16
    dma = pltpu.SemaphoreType.DMA
    any_space = pl.BlockSpec(memory_space=pl.ANY)
    mix, drec, gathered = pl.pallas_call(
        functools.partial(kernel, factor),
        out_shape=(
            pltpu.VMEM((16, 512, 128), BF), pltpu.VMEM((16, 512, 128), BF), pltpu.VMEM((2, members, height, 128), BF)
        ),
        in_specs=[pl.BlockSpec(memory_space=pltpu.HBM)] * 4,
        out_specs=(pl.BlockSpec(memory_space=pltpu.VMEM),) * 3,
        scratch_shapes=[
            pltpu.VMEM((16, 512, 128), BF),
            pltpu.VMEM((24, 512, 128), BF),
            pltpu.VMEM((24, 512, 128), BF),
            pltpu.VMEM((36, 128, 256), BF),
            pltpu.VMEM((36, 256, 128), BF),
            pltpu.VMEM((12, 256, 512), BF),
            pltpu.VMEM((36, 128, 256), BF),
            pltpu.VMEM((32, 128, 256), F32),
            pltpu.VMEM((2, 9, 128, 128), BF),
            pltpu.VMEM((4, 1280, 256), BF),
            pltpu.VMEM((2, 1280, 256), F32),
            pltpu.VMEM((2, 9, 128, 128), F32),
            pltpu.VMEM((9, 128, 128), F32),
            pltpu.VMEM((members, height, 128), WIRE),
            pltpu.VMEM((members, height, 128), WIRE),
            pltpu.VMEM((nf, used, 128), F32),
            dma((8,)),
            dma((2, CHUNKS)), dma((2, CHUNKS)), dma((2, CHUNKS)), dma((2, CHUNKS)),
            dma((2, 1)), dma((2, 1)), dma((2, 1)), dma((2, 1)),
            dma((2,)), dma((members,)), dma((members,)), dma((nf,)), dma((nf,)), dma((members,)), dma((members,)),
            dma((2,)),
        ],
        compiler_params=pltpu.CompilerParams(
            collective_id=0, has_side_effects=True, vmem_limit_bytes=48 << 20
        ),
        cost_estimate=pl.CostEstimate(flops=16 * 10**9, bytes_accessed=10**7, transcendentals=10**6),
        name="block",
    )(*(pltpu.with_memory_space_constraint(a, pltpu.HBM) for a in (records[0], time_weight, fibre_weight, cotangent[0])))

    def store(mix, drec, gathered, mixed, d_records, grad_time, grad_fibre, staged, sem):
        copies = [pltpu.make_async_copy(mix, mixed, sem.at[0]), pltpu.make_async_copy(drec, d_records, sem.at[1])]
        for c in copies:
            c.start()
        rows = 128 // members
        for i, out in enumerate((grad_time, grad_fibre)):
            for s in range(members):
                staged[i, :, rows * s : rows * s + rows] = gathered[i, s].astype(F32)[:used].reshape(9, rows, 128)
            copies.append(pltpu.make_async_copy(staged.at[i], out, sem.at[2 + i]))
            copies[-1].start()
        for c in copies:
            c.wait()

    field = jax.ShapeDtypeStruct((16, 512, 128), BF)
    grad = jax.ShapeDtypeStruct((9, 128, 128), F32)
    mixed, d_records, grad_time, grad_fibre = pl.pallas_call(
        store,
        out_shape=(field, field, grad, grad),
        in_specs=[any_space, any_space, pl.BlockSpec(memory_space=pltpu.VMEM)],
        out_specs=(any_space,) * 4,
        scratch_shapes=[pltpu.VMEM((2, 9, 128, 128), F32), dma((4,))],
        compiler_params=pltpu.CompilerParams(vmem_limit_bytes=8 << 20),
        cost_estimate=pl.CostEstimate(flops=0, bytes_accessed=10**7, transcendentals=0),
        name="store",
    )(mix, drec, gathered)
    return mixed[None], d_records[None], grad_time, grad_fibre


def solution(mesh):
    spec = P("rep", "fibre", "tm", None)
    total = 8 * 64 * 2048
    return jax.shard_map(
        functools.partial(shards, float(total) ** -0.5),
        mesh=mesh,
        in_specs=(spec, P(), P(), spec),
        out_specs=(spec, spec, P(), P()),
        check_vma=False,
    )
```

```python
import functools

import jax
import jax.numpy as jnp
from jax import lax
from jax.experimental import pallas as pl
from jax.experimental.pallas import tpu as pltpu
from jax.sharding import PartitionSpec as P

MESH = pl.DeviceIdType.MESH
BF, F32 = jnp.bfloat16, jnp.float32
TILE = 4
SPANS = (slice(0, 256), slice(256, 512))
CHUNKS = len(SPANS)
EDGES = (0, 1, 6, 7)
WIRE = BF


def dot(a, b):
    return jnp.dot(a, b, preferred_element_type=F32)


def loop(low, high, body):
    lax.fori_loop(low, high, lambda i, c: (body(i), c)[1], 0, unroll=high - low)


def aligned(index, size):
    return pl.ds(pl.multiple_of(index * size, size), size)


def pair_weights(dst, block):
    zero = jnp.zeros((128, 128), BF)
    for b in range(5):
        top, low = slice(256 * b, 256 * b + 128), slice(256 * b + 128, 256 * b + 256)
        dst[top, 0:128] = block(2 * b)
        dst[top, 128:256] = block(2 * b - 1) if b > 0 else zero
        dst[low, 0:128] = block(2 * b + 1) if b < 4 else zero
        dst[low, 128:256] = block(2 * b)


def to_time_pairs(src, q):
    v = src[:, aligned(q, 16), :].astype(F32)
    lo, hi = v[:, 0:8].reshape(128, 128), v[:, 8:16].reshape(128, 128)
    return jnp.concatenate([lo, hi], axis=1).astype(BF)


def natural(y):
    y = y.reshape(16, 8, 256)
    return jnp.concatenate([y[:, :, :128], y[:, :, 128:]], axis=1)


def time_conv(src, w, q0):
    lhs = [src[pl.ds(q0 + b, TILE)].reshape(TILE * 128, 256) for b in range(5)]
    return dot(jnp.concatenate(lhs, axis=1), w[...])


def do_hidden(xt, w, h, slope, q0):
    y = time_conv(xt, w, q0)
    s = 0.5 * jnp.tanh(0.5 * y) + 0.5
    hid = y * s
    slope[pl.ds(q0, TILE)] = (s + hid * (1.0 - s)).reshape(TILE, 128, 256)
    for j in range(TILE):
        h[4:20, aligned(q0 + j, 16), :] = natural(hid[128 * j : 128 * j + 128]).astype(BF)


def fibre_rows(src, items):
    return jnp.concatenate(
        [jnp.concatenate([src[2 * p + i, at] for i in range(10)], axis=1) for p, at in items], axis=0
    )


def split_rows(y, items):
    low = 0
    for p, at in items:
        size = at.stop - at.start
        yield p, at, size, y[low : low + size]
        low += size


def do_d_pre(g, w, slope, dp, items):
    for p, at, size, z in split_rows(dot(fibre_rows(g, items), w[...]), items):
        count, q0 = size // 16, at.start // 16
        z = z.reshape(size // 8, 8, 256)
        z = jnp.concatenate([z[:, :, :128], z[:, :, 128:]], axis=1).reshape(count, 2, 16, 128)
        z = jnp.concatenate([z[:, 0], z[:, 1]], axis=2)
        rows = aligned(p, 16)
        dp[2 + q0 : 2 + q0 + count, rows, :] = (z * slope[q0 : q0 + count, rows, :]).astype(BF)


def do_grad_fibre(gt, h, acc, items):
    lhs = [gt[pl.ds(p, 5), :, at].reshape(1280, at.stop - at.start) for p, at in items]
    rhs = [jnp.concatenate([h[4 + 2 * p, at], h[5 + 2 * p, at]], axis=1) for p, at in items]
    acc[...] += dot(jnp.concatenate(lhs, axis=1), jnp.concatenate(rhs, axis=0))


def do_mixed(h, w, x, out, items):
    for p, at, size, z in split_rows(dot(fibre_rows(h, items), w[...]), items):
        out[2 * p, at] = (x[2 * p, at].astype(F32) + z[:, :128]).astype(BF)
        out[2 * p + 1, at] = (x[2 * p + 1, at].astype(F32) + z[:, 128:]).astype(BF)


def do_grad_time(xtt, dp, acc, q0, count):
    lhs = [jnp.concatenate([xtt[q0 + b + j] for j in range(count)], axis=1) for b in range(5)]
    acc[...] += dot(jnp.concatenate(lhs, axis=0), dp[pl.ds(2 + q0, count)].reshape(count * 128, 256))


def do_d_records(dp, w, g, out, q0):
    y = time_conv(dp, w, q0)
    for j in range(TILE):
        at = aligned(q0 + j, 16)
        out[:, at, :] = (g[4:20, at, :].astype(F32) + natural(y[128 * j : 128 * j + 128])).astype(BF)


def fold(acc, grads):
    def part(i, b, e, d):
        return acc[i, 256 * b + 128 * e : 256 * b + 128 * e + 128, 128 * d : 128 * d + 128]

    for k in range(9):
        if k % 2 == 0:
            low, high = k // 2, (8 - k) // 2
            grads[0, k] = part(0, low, 0, 0) + part(0, low, 1, 1)
            grads[1, k] = (part(1, high, 0, 0) + part(1, high, 1, 1)).T
        else:
            grads[0, k] = part(0, (k - 1) // 2, 1, 0) + part(0, (k + 1) // 2, 0, 1)
            grads[1, k] = (part(1, (9 - k) // 2, 0, 1) + part(1, (7 - k) // 2, 1, 0)).T


def kernel(factor, x_hbm, tw_hbm, fw_hbm, g_hbm, mix, drec, gathered,
           x, g, h, xt, xtt, gt, dp, slope, wraw, big, acc, grads, other, parts, inbox, planes,
           lsem, gsend, grecv, hsend, hrecv, xsend, xrecv, dsend, drecv, asem, bsend, brecv, csend, crecv, esend, erecv,
           fsem):
    fi, ti, ri = lax.axis_index("fibre"), lax.axis_index("tm"), lax.axis_index("rep")
    nf, nt, nr = lax.axis_size("fibre"), lax.axis_size("tm"), lax.axis_size("rep")
    core = lax.rem(ti, 2)
    members = (nt // 2) * nr
    me = lax.div(ti, 2) * nr + ri
    rows = 128 // members
    used = 9 * rows

    offsets = sorted(range(1, members), key=lambda d: -sum(min(i, 4 - i) for i in (d // 4, d % 4)))

    def moved(d, sign):
        return 4 * lax.rem(me // 4 + sign * (d // 4) + members, members // 4) + lax.rem(me % 4 + sign * (d % 4) + 4, 4)

    def member(index):
        return {"tm": 2 * lax.div(index, nr) + core, "rep": lax.rem(index, nr)}

    def shifted(axis, index, count, step):
        return {axis: lax.rem(index + step + count, count)}

    partner = {"tm": ti + 1 - 2 * core}

    barrier = pltpu.get_barrier_semaphore()
    others = [shifted("fibre", fi, nf, d) for d in range(1, nf)]
    others += [shifted("tm", ti, nt, d) for d in (1, -1)]
    others = [member(moved(d, 1)) for d in offsets] + others
    for d in others:
        pl.semaphore_signal(barrier, inc=1, device_id=d, device_id_type=MESH)

    x_edges = [pltpu.make_async_copy(x_hbm.at[:, at, :], x.at[:, at, :], lsem.at[i])
               for i, at in enumerate((slice(0, 32), slice(480, 512)))]
    x_rest = pltpu.make_async_copy(x_hbm.at[:, 32:480, :], x.at[:, 32:480, :], lsem.at[2])
    w_time = pltpu.make_async_copy(tw_hbm, wraw.at[0], lsem.at[3])
    w_fibre = pltpu.make_async_copy(fw_hbm, wraw.at[1], lsem.at[4])
    g_load = pltpu.make_async_copy(g_hbm, g.at[4:20], lsem.at[5])
    for c in (*x_edges, w_time, x_rest, w_fibre, g_load):
        c.start()

    class Halo:
        def __init__(self, axis, index, count, pieces, send, recv):
            self.has = (index < count - 1, index > 0)
            self.copies = [
                [pltpu.make_async_remote_copy(
                    src_ref=src, dst_ref=dst, send_sem=send.at[side, i], recv_sem=recv.at[side, i],
                    device_id=shifted(axis, index, count, 1 - 2 * side), device_id_type=MESH)
                 for side, (src, dst) in enumerate(piece)]
                for i, piece in enumerate(pieces)]

        def start(self, i):
            for side in range(2):
                pl.when(self.has[side])(self.copies[i][side].start)

        def wait_recv(self, i):
            for side in range(2):
                pl.when(self.has[1 - side])(self.copies[i][side].wait_recv)

        def wait_send(self, i):
            for side in range(2):
                pl.when(self.has[side])(self.copies[i][side].wait_send)

    g_halo = Halo("fibre", fi, nf, [
        ((g_hbm.at[12:16, at, :], g.at[0:4, at, :]), (g_hbm.at[0:4, at, :], g.at[20:24, at, :])) for at in SPANS
    ], gsend, grecv)
    h_halo = Halo("fibre", fi, nf, [
        ((h.at[16:20, at, :], h.at[0:4, at, :]), (h.at[4:8, at, :], h.at[20:24, at, :])) for at in SPANS
    ], hsend, hrecv)
    x_halo = Halo("tm", ti, nt, [((xt.at[32:34], xt.at[0:2]), (xt.at[2:4], xt.at[34:36]))], xsend, xrecv)
    d_halo = Halo("tm", ti, nt, [((dp.at[32:34], dp.at[0:2]), (dp.at[2:4], dp.at[34:36]))], dsend, drecv)
    def build(q):
        v = to_time_pairs(x, q)
        xt[q + 2] = v
        xtt[q + 2] = v.T

    for c in x_edges:
        c.wait()
    for q in (0, 1, 30, 31):
        build(q)
    pl.semaphore_wait(barrier, len(others))
    x_halo.start(0)
    for i in range(CHUNKS):
        g_halo.start(i)

    for edge, at, time_at in ((0, slice(0, 4), slice(0, 2)), (1, slice(20, 24), slice(34, 36))):
        @pl.when((fi == 0) if edge == 0 else (fi == nf - 1))
        def _(at=at):
            g[at] = jnp.zeros((4, 512, 128), BF)
            h[at] = jnp.zeros((4, 512, 128), BF)

        @pl.when((ti == 0) if edge == 0 else (ti == nt - 1))
        def _(at=time_at):
            xt[at] = jnp.zeros((2, 128, 256), BF)
            dp[at] = jnp.zeros((2, 128, 256), BF)

    w_time.wait()
    pair_weights(big.at[0], lambda k: wraw[0, k])
    x_rest.wait()
    loop(2, 30, build)
    last = 32 // TILE - 1
    loop(1, last, lambda i: do_hidden(xt, big.at[0], h, slope, i * TILE))

    w_fibre.wait()
    pair_weights(big.at[1], lambda k: wraw[1, 8 - k].T)
    pair_weights(big.at[2], lambda k: wraw[1, k])
    pair_weights(big.at[3], lambda k: wraw[0, 8 - k].T)

    g_load.wait()

    def turn(p, spans):
        for at in spans:
            gt[p, :, at] = jnp.concatenate([g[2 * p, at], g[2 * p + 1, at]], axis=1).T

    acc[...] = jnp.zeros(acc.shape, F32)
    quarters = [slice(128 * i, 128 * i + 128) for i in range(4)]
    loop(2, 10, lambda p: turn(p, quarters))
    inner, outer = (slice(128, 384),), (quarters[0], quarters[3])
    loop(2, 6, lambda p: do_d_pre(g, big.at[1], slope, dp, [(p, at) for at in inner]))
    loop(2, 6, lambda p: do_grad_fibre(gt, h, acc.at[1], [(p, at) for at in inner]))

    x_halo.wait_recv(0)
    for q in (0, 1, 34, 35):
        xtt[q] = xt[q].T
    do_hidden(xt, big.at[0], h, slope, last * TILE)
    do_hidden(xt, big.at[0], h, slope, 0)
    loop(2, 6, lambda p: do_d_pre(g, big.at[1], slope, dp, [(p, at) for at in outer]))
    loop(2, 6, lambda p: do_grad_fibre(gt, h, acc.at[1], [(p, at) for at in outer]))

    for i, at in enumerate(SPANS):
        g_halo.wait_recv(i)
        if i == CHUNKS - 1:
            for j in range(CHUNKS):
                h_halo.start(j)
        items = [(p, at) for p in EDGES]
        do_d_pre(g, big.at[1], slope, dp, items)
        if i == CHUNKS - 1:
            d_halo.start(0)
        for p in (0, 1, 10, 11):
            turn(p, [at])
        do_grad_fibre(gt, h, acc.at[1], items)
        loop(at.start // 64, at.stop // 64, lambda q: do_grad_time(xtt, dp, acc.at[0], 4 * q, 4))
    fold(acc, grads)

    swap = pltpu.make_async_remote_copy(
        src_ref=grads.at[1 - core], dst_ref=other, send_sem=asem.at[0], recv_sem=asem.at[1],
        device_id=partner, device_id_type=MESH)
    swap.start()
    loop(2, 6, lambda p: do_mixed(h, big.at[2], x, mix, [(p, slice(0, 512))]))
    swap.wait_recv()

    pad = jnp.zeros((parts.shape[1] - used, 128), F32) if parts.shape[1] > used else None

    def padded(v):
        return v if pad is None else jnp.concatenate([v, pad], axis=0)

    for s in range(members):
        at = slice(rows * s, rows * s + rows)
        parts[s] = padded((grads[core, :, at] + other[:, at]).reshape(used, 128)).astype(WIRE)
    mine = aligned(me, rows)
    own = (grads[core, :, mine] + other[:, mine]).reshape(used, 128)
    scatter = []
    for d in offsets:
        to = moved(d, 1)
        scatter.append(pltpu.make_async_remote_copy(
            src_ref=parts.at[to], dst_ref=inbox.at[d], send_sem=bsend.at[d], recv_sem=brecv.at[d],
            device_id=member(to), device_id_type=MESH))
    for c in scatter:
        c.start()

    loop(1, last, lambda i: do_d_records(dp, big.at[3], g, drec, i * TILE))
    for d, c in zip(offsets, scatter):
        c.wait_recv()
        own = own + inbox[d].astype(F32)[:used]
    planes[fi] = own
    spread = []
    for d in range(1, nf):
        to = lax.rem(fi + d, nf)
        spread.append(pltpu.make_async_remote_copy(
            src_ref=planes.at[fi], dst_ref=planes.at[fi], send_sem=csend.at[d], recv_sem=crecv.at[d],
            device_id={"fibre": to}, device_id_type=MESH))
    for c in spread:
        c.start()

    d_halo.wait_recv(0)
    do_d_records(dp, big.at[3], g, drec, last * TILE)
    do_d_records(dp, big.at[3], g, drec, 0)
    for d in range(1, nf):
        source = lax.rem(fi - d + nf, nf)
        pltpu.make_async_remote_copy(
            src_ref=planes.at[source], dst_ref=planes.at[source], send_sem=csend.at[d], recv_sem=crecv.at[d],
            device_id={"fibre": source}, device_id_type=MESH).wait_recv()
    total = planes[0]
    for i in range(1, nf):
        total = total + planes[i]
    gathered[core, me] = padded(total * factor).astype(BF)
    def piece(which, part, to):
        return pltpu.make_async_remote_copy(
            src_ref=gathered.at[which, part], dst_ref=gathered.at[which, part], send_sem=esend.at[to],
            recv_sem=erecv.at[part], device_id=member(to), device_id_type=MESH)

    pl.when(me != 0)(piece(core, me, 0).start)
    for d in offsets:
        to = moved(d, 1)
        pl.when(to != 0)(piece(core, me, to).start)

    for i in range(CHUNKS):
        h_halo.wait_recv(i)
        do_mixed(h, big.at[2], x, mix, [(p, SPANS[i]) for p in EDGES])

    for s in range(members):
        pl.when(me != s)(piece(core, s, me).wait_recv)

    def forward(which):
        return pltpu.make_async_remote_copy(
            src_ref=gathered.at[which], dst_ref=gathered.at[which], send_sem=fsem.at[0],
            recv_sem=fsem.at[1], device_id=partner, device_id_type=MESH)

    forward(core).start()
    forward(1 - core).wait_recv()

    forward(core).wait_send()
    swap.wait_send()
    for c in (*scatter, *spread):
        c.wait_send()
    for s in range(members):
        pl.when(me != s)(piece(core, me, s).wait_send)
    for halo, count in ((g_halo, CHUNKS), (h_halo, CHUNKS), (x_halo, 1), (d_halo, 1)):
        for i in range(count):
            halo.wait_send(i)


def shards(factor, records, time_weight, fibre_weight, cotangent):
    nf, nt, nr = lax.axis_size("fibre"), lax.axis_size("tm"), lax.axis_size("rep")
    members = (nt // 2) * nr
    used = 9 * (128 // members)
    height = -(-used // 16) * 16
    dma = pltpu.SemaphoreType.DMA
    any_space = pl.BlockSpec(memory_space=pl.ANY)
    mix, drec, gathered = pl.pallas_call(
        functools.partial(kernel, factor),
        out_shape=(
            pltpu.VMEM((16, 512, 128), BF), pltpu.VMEM((16, 512, 128), BF), pltpu.VMEM((2, members, height, 128), BF)
        ),
        in_specs=[pl.BlockSpec(memory_space=pltpu.HBM)] * 4,
        out_specs=(pl.BlockSpec(memory_space=pltpu.VMEM),) * 3,
        scratch_shapes=[
            pltpu.VMEM((16, 512, 128), BF),
            pltpu.VMEM((24, 512, 128), BF),
            pltpu.VMEM((24, 512, 128), BF),
            pltpu.VMEM((36, 128, 256), BF),
            pltpu.VMEM((36, 256, 128), BF),
            pltpu.VMEM((12, 256, 512), BF),
            pltpu.VMEM((36, 128, 256), BF),
            pltpu.VMEM((32, 128, 256), F32),
            pltpu.VMEM((2, 9, 128, 128), BF),
            pltpu.VMEM((4, 1280, 256), BF),
            pltpu.VMEM((2, 1280, 256), F32),
            pltpu.VMEM((2, 9, 128, 128), F32),
            pltpu.VMEM((9, 128, 128), F32),
            pltpu.VMEM((members, height, 128), WIRE),
            pltpu.VMEM((members, height, 128), WIRE),
            pltpu.VMEM((nf, used, 128), F32),
            dma((8,)),
            dma((2, CHUNKS)), dma((2, CHUNKS)), dma((2, CHUNKS)), dma((2, CHUNKS)),
            dma((2, 1)), dma((2, 1)), dma((2, 1)), dma((2, 1)),
            dma((2,)), dma((members,)), dma((members,)), dma((nf,)), dma((nf,)), dma((members,)), dma((members,)),
            dma((2,)),
        ],
        compiler_params=pltpu.CompilerParams(
            collective_id=0, has_side_effects=True, vmem_limit_bytes=48 << 20
        ),
        cost_estimate=pl.CostEstimate(flops=16 * 10**9, bytes_accessed=10**7, transcendentals=10**6),
        name="block",
    )(*(pltpu.with_memory_space_constraint(a, pltpu.HBM) for a in (records[0], time_weight, fibre_weight, cotangent[0])))

    def store(mix, drec, gathered, mixed, d_records, grad_time, grad_fibre, staged, sem):
        copies = [pltpu.make_async_copy(mix, mixed, sem.at[0]), pltpu.make_async_copy(drec, d_records, sem.at[1])]
        for c in copies:
            c.start()
        rows = 128 // members
        for i, out in enumerate((grad_time, grad_fibre)):
            for s in range(members):
                staged[i, :, rows * s : rows * s + rows] = gathered[i, s].astype(F32)[:used].reshape(9, rows, 128)
            copies.append(pltpu.make_async_copy(staged.at[i], out, sem.at[2 + i]))
            copies[-1].start()
        for c in copies:
            c.wait()

    field = jax.ShapeDtypeStruct((16, 512, 128), BF)
    grad = jax.ShapeDtypeStruct((9, 128, 128), F32)
    mixed, d_records, grad_time, grad_fibre = pl.pallas_call(
        store,
        out_shape=(field, field, grad, grad),
        in_specs=[any_space, any_space, pl.BlockSpec(memory_space=pltpu.VMEM)],
        out_specs=(any_space,) * 4,
        scratch_shapes=[pltpu.VMEM((2, 9, 128, 128), F32), dma((4,))],
        compiler_params=pltpu.CompilerParams(vmem_limit_bytes=8 << 20),
        cost_estimate=pl.CostEstimate(flops=0, bytes_accessed=10**7, transcendentals=0),
        name="store",
    )(mix, drec, gathered)
    return mixed[None], d_records[None], grad_time, grad_fibre


def solution(mesh):
    spec = P("rep", "fibre", "tm", None)
    total = 8 * 64 * 2048
    return jax.shard_map(
        functools.partial(shards, float(total) ** -0.5),
        mesh=mesh,
        in_specs=(spec, P(), P(), spec),
        out_specs=(spec, spec, P(), P()),
        check_vma=False,
    )
```

```python
import functools

import jax
import jax.numpy as jnp
from jax import lax
from jax.experimental import pallas as pl
from jax.experimental.pallas import tpu as pltpu
from jax.sharding import PartitionSpec as P

MESH = pl.DeviceIdType.MESH
BF, F32 = jnp.bfloat16, jnp.float32
TILE = 4
SPANS = (slice(0, 256), slice(256, 512))
CHUNKS = len(SPANS)
EDGES = (0, 1, 6, 7)
WIRE = BF


def dot(a, b):
    return jnp.dot(a, b, preferred_element_type=F32)


def loop(low, high, body):
    lax.fori_loop(low, high, lambda i, c: (body(i), c)[1], 0, unroll=high - low)


def aligned(index, size):
    return pl.ds(pl.multiple_of(index * size, size), size)


def pair_weights(dst, block):
    zero = jnp.zeros((128, 128), BF)
    for b in range(5):
        top, low = slice(256 * b, 256 * b + 128), slice(256 * b + 128, 256 * b + 256)
        dst[top, 0:128] = block(2 * b)
        dst[top, 128:256] = block(2 * b - 1) if b > 0 else zero
        dst[low, 0:128] = block(2 * b + 1) if b < 4 else zero
        dst[low, 128:256] = block(2 * b)


def to_time_pairs(src, q):
    v = src[:, aligned(q, 16), :].astype(F32)
    lo, hi = v[:, 0:8].reshape(128, 128), v[:, 8:16].reshape(128, 128)
    return jnp.concatenate([lo, hi], axis=1).astype(BF)


def natural(y):
    y = y.reshape(16, 8, 256)
    return jnp.concatenate([y[:, :, :128], y[:, :, 128:]], axis=1)


def time_conv(src, w, q0):
    lhs = [src[pl.ds(q0 + b, TILE)].reshape(TILE * 128, 256) for b in range(5)]
    return dot(jnp.concatenate(lhs, axis=1), w[...])


def do_hidden(xt, w, h, slope, q0):
    y = time_conv(xt, w, q0)
    s = 0.5 * jnp.tanh(0.5 * y) + 0.5
    hid = y * s
    slope[pl.ds(q0, TILE)] = (s + hid * (1.0 - s)).reshape(TILE, 128, 256)
    for j in range(TILE):
        h[4:20, aligned(q0 + j, 16), :] = natural(hid[128 * j : 128 * j + 128]).astype(BF)


def fibre_rows(src, items):
    return jnp.concatenate(
        [jnp.concatenate([src[2 * p + i, at] for i in range(10)], axis=1) for p, at in items], axis=0
    )


def split_rows(y, items):
    low = 0
    for p, at in items:
        size = at.stop - at.start
        yield p, at, size, y[low : low + size]
        low += size


def do_d_pre(g, w, slope, dp, items):
    for p, at, size, z in split_rows(dot(fibre_rows(g, items), w[...]), items):
        count, q0 = size // 16, at.start // 16
        z = z.reshape(size // 8, 8, 256)
        z = jnp.concatenate([z[:, :, :128], z[:, :, 128:]], axis=1).reshape(count, 2, 16, 128)
        z = jnp.concatenate([z[:, 0], z[:, 1]], axis=2)
        rows = aligned(p, 16)
        dp[2 + q0 : 2 + q0 + count, rows, :] = (z * slope[q0 : q0 + count, rows, :]).astype(BF)


def do_grad_fibre(gt, h, acc, items):
    lhs = [gt[pl.ds(p, 5), :, at].reshape(1280, at.stop - at.start) for p, at in items]
    rhs = [jnp.concatenate([h[4 + 2 * p, at], h[5 + 2 * p, at]], axis=1) for p, at in items]
    acc[...] += dot(jnp.concatenate(lhs, axis=1), jnp.concatenate(rhs, axis=0))


def do_mixed(h, w, x, out, items):
    for p, at, size, z in split_rows(dot(fibre_rows(h, items), w[...]), items):
        out[2 * p, at] = (x[2 * p, at].astype(F32) + z[:, :128]).astype(BF)
        out[2 * p + 1, at] = (x[2 * p + 1, at].astype(F32) + z[:, 128:]).astype(BF)


def do_grad_time(xtt, dp, acc, q0, count):
    lhs = [jnp.concatenate([xtt[q0 + b + j] for j in range(count)], axis=1) for b in range(5)]
    acc[...] += dot(jnp.concatenate(lhs, axis=0), dp[pl.ds(2 + q0, count)].reshape(count * 128, 256))


def do_d_records(dp, w, g, out, q0):
    y = time_conv(dp, w, q0)
    for j in range(TILE):
        at = aligned(q0 + j, 16)
        out[:, at, :] = (g[4:20, at, :].astype(F32) + natural(y[128 * j : 128 * j + 128])).astype(BF)


def fold(acc, grads):
    def part(i, b, e, d):
        return acc[i, 256 * b + 128 * e : 256 * b + 128 * e + 128, 128 * d : 128 * d + 128]

    for k in range(9):
        if k % 2 == 0:
            low, high = k // 2, (8 - k) // 2
            grads[0, k] = part(0, low, 0, 0) + part(0, low, 1, 1)
            grads[1, k] = (part(1, high, 0, 0) + part(1, high, 1, 1)).T
        else:
            grads[0, k] = part(0, (k - 1) // 2, 1, 0) + part(0, (k + 1) // 2, 0, 1)
            grads[1, k] = (part(1, (9 - k) // 2, 0, 1) + part(1, (7 - k) // 2, 1, 0)).T


def kernel(factor, x_hbm, tw_hbm, fw_hbm, g_hbm, mix, drec, gathered,
           x, g, h, xt, xtt, gt, dp, slope, wraw, big, acc, grads, other, parts, inbox, planes,
           lsem, gsend, grecv, hsend, hrecv, xsend, xrecv, dsend, drecv, asem, bsend, brecv, csend, crecv, esend, erecv,
           fsem):
    fi, ti, ri = lax.axis_index("fibre"), lax.axis_index("tm"), lax.axis_index("rep")
    nf, nt, nr = lax.axis_size("fibre"), lax.axis_size("tm"), lax.axis_size("rep")
    core = lax.rem(ti, 2)
    members = (nt // 2) * nr
    me = lax.div(ti, 2) * nr + ri
    rows = 128 // members
    used = 9 * rows

    offsets = sorted(range(1, members), key=lambda d: -sum(min(i, 4 - i) for i in (d // 4, d % 4)))

    def moved(d, sign):
        return 4 * lax.rem(me // 4 + sign * (d // 4) + members, members // 4) + lax.rem(me % 4 + sign * (d % 4) + 4, 4)

    def member(index):
        return {"tm": 2 * lax.div(index, nr) + core, "rep": lax.rem(index, nr)}

    def shifted(axis, index, count, step):
        return {axis: lax.rem(index + step + count, count)}

    partner = {"tm": ti + 1 - 2 * core}

    barrier = pltpu.get_barrier_semaphore()
    others = [shifted("fibre", fi, nf, d) for d in range(1, nf)]
    others += [shifted("tm", ti, nt, d) for d in (1, -1)]
    others = [member(moved(d, 1)) for d in offsets] + others
    for d in others:
        pl.semaphore_signal(barrier, inc=1, device_id=d, device_id_type=MESH)

    x_edges = [pltpu.make_async_copy(x_hbm.at[:, at, :], x.at[:, at, :], lsem.at[i])
               for i, at in enumerate((slice(0, 32), slice(480, 512)))]
    x_rest = pltpu.make_async_copy(x_hbm.at[:, 32:480, :], x.at[:, 32:480, :], lsem.at[2])
    w_time = pltpu.make_async_copy(tw_hbm, wraw.at[0], lsem.at[3])
    w_fibre = pltpu.make_async_copy(fw_hbm, wraw.at[1], lsem.at[4])
    g_load = pltpu.make_async_copy(g_hbm, g.at[4:20], lsem.at[5])
    for c in (*x_edges, w_time, x_rest, w_fibre, g_load):
        c.start()

    class Halo:
        def __init__(self, axis, index, count, pieces, send, recv):
            self.has = (index < count - 1, index > 0)
            self.copies = [
                [pltpu.make_async_remote_copy(
                    src_ref=src, dst_ref=dst, send_sem=send.at[side, i], recv_sem=recv.at[side, i],
                    device_id=shifted(axis, index, count, 1 - 2 * side), device_id_type=MESH)
                 for side, (src, dst) in enumerate(piece)]
                for i, piece in enumerate(pieces)]

        def start(self, i):
            for side in range(2):
                pl.when(self.has[side])(self.copies[i][side].start)

        def wait_recv(self, i):
            for side in range(2):
                pl.when(self.has[1 - side])(self.copies[i][side].wait_recv)

        def wait_send(self, i):
            for side in range(2):
                pl.when(self.has[side])(self.copies[i][side].wait_send)

    g_halo = Halo("fibre", fi, nf, [
        ((g_hbm.at[12:16, at, :], g.at[0:4, at, :]), (g_hbm.at[0:4, at, :], g.at[20:24, at, :])) for at in SPANS
    ], gsend, grecv)
    h_halo = Halo("fibre", fi, nf, [
        ((h.at[16:20, at, :], h.at[0:4, at, :]), (h.at[4:8, at, :], h.at[20:24, at, :])) for at in SPANS
    ], hsend, hrecv)
    x_halo = Halo("tm", ti, nt, [((xt.at[32:34], xt.at[0:2]), (xt.at[2:4], xt.at[34:36]))], xsend, xrecv)
    d_halo = Halo("tm", ti, nt, [((dp.at[32:34], dp.at[0:2]), (dp.at[2:4], dp.at[34:36]))], dsend, drecv)
    def build(q):
        v = to_time_pairs(x, q)
        xt[q + 2] = v
        xtt[q + 2] = v.T

    for c in x_edges:
        c.wait()
    for q in (0, 1, 30, 31):
        build(q)
    pl.semaphore_wait(barrier, len(others))
    x_halo.start(0)
    for i in range(CHUNKS):
        g_halo.start(i)

    for edge, at, time_at in ((0, slice(0, 4), slice(0, 2)), (1, slice(20, 24), slice(34, 36))):
        @pl.when((fi == 0) if edge == 0 else (fi == nf - 1))
        def _(at=at):
            g[at] = jnp.zeros((4, 512, 128), BF)
            h[at] = jnp.zeros((4, 512, 128), BF)

        @pl.when((ti == 0) if edge == 0 else (ti == nt - 1))
        def _(at=time_at):
            xt[at] = jnp.zeros((2, 128, 256), BF)
            dp[at] = jnp.zeros((2, 128, 256), BF)

    w_time.wait()
    pair_weights(big.at[0], lambda k: wraw[0, k])
    x_rest.wait()
    loop(2, 30, build)
    last = 32 // TILE - 1
    loop(1, last, lambda i: do_hidden(xt, big.at[0], h, slope, i * TILE))

    w_fibre.wait()
    pair_weights(big.at[1], lambda k: wraw[1, 8 - k].T)
    pair_weights(big.at[2], lambda k: wraw[1, k])
    pair_weights(big.at[3], lambda k: wraw[0, 8 - k].T)

    g_load.wait()

    def turn(p, spans):
        for at in spans:
            gt[p, :, at] = jnp.concatenate([g[2 * p, at], g[2 * p + 1, at]], axis=1).T

    acc[...] = jnp.zeros(acc.shape, F32)
    quarters = [slice(128 * i, 128 * i + 128) for i in range(4)]
    loop(2, 10, lambda p: turn(p, quarters))
    inner, outer = (slice(128, 384),), (quarters[0], quarters[3])
    loop(2, 6, lambda p: do_d_pre(g, big.at[1], slope, dp, [(p, at) for at in inner]))
    loop(2, 6, lambda p: do_grad_fibre(gt, h, acc.at[1], [(p, at) for at in inner]))

    x_halo.wait_recv(0)
    for q in (0, 1, 34, 35):
        xtt[q] = xt[q].T
    do_hidden(xt, big.at[0], h, slope, last * TILE)
    do_hidden(xt, big.at[0], h, slope, 0)
    loop(2, 6, lambda p: do_d_pre(g, big.at[1], slope, dp, [(p, at) for at in outer]))
    loop(2, 6, lambda p: do_grad_fibre(gt, h, acc.at[1], [(p, at) for at in outer]))

    for i, at in enumerate(SPANS):
        g_halo.wait_recv(i)
        if i == CHUNKS - 1:
            for j in range(CHUNKS):
                h_halo.start(j)
        items = [(p, at) for p in EDGES]
        do_d_pre(g, big.at[1], slope, dp, items)
        if i == CHUNKS - 1:
            d_halo.start(0)
        for p in (0, 1, 10, 11):
            turn(p, [at])
        do_grad_fibre(gt, h, acc.at[1], items)
        loop(at.start // 64, at.stop // 64, lambda q: do_grad_time(xtt, dp, acc.at[0], 4 * q, 4))
    fold(acc, grads)

    swap = pltpu.make_async_remote_copy(
        src_ref=grads.at[1 - core], dst_ref=other, send_sem=asem.at[0], recv_sem=asem.at[1],
        device_id=partner, device_id_type=MESH)
    swap.start()
    loop(2, 6, lambda p: do_mixed(h, big.at[2], x, mix, [(p, slice(0, 512))]))
    swap.wait_recv()

    pad = jnp.zeros((parts.shape[1] - used, 128), F32) if parts.shape[1] > used else None

    def padded(v):
        return v if pad is None else jnp.concatenate([v, pad], axis=0)

    mine = aligned(me, rows)
    own = (grads[core, :, mine] + other[:, mine]).reshape(used, 128)
    scatter = []
    for d in offsets:
        to = moved(d, 1)
        at = aligned(to, rows)
        parts[to] = padded((grads[core, :, at] + other[:, at]).reshape(used, 128)).astype(WIRE)
        scatter.append(pltpu.make_async_remote_copy(
            src_ref=parts.at[to], dst_ref=inbox.at[d], send_sem=bsend.at[d], recv_sem=brecv.at[d],
            device_id=member(to), device_id_type=MESH))
        scatter[-1].start()

    loop(1, last, lambda i: do_d_records(dp, big.at[3], g, drec, i * TILE))
    for d, c in zip(offsets, scatter):
        c.wait_recv()
        own = own + inbox[d].astype(F32)[:used]
    planes[fi] = own
    spread = []
    for d in range(1, nf):
        to = lax.rem(fi + d, nf)
        spread.append(pltpu.make_async_remote_copy(
            src_ref=planes.at[fi], dst_ref=planes.at[fi], send_sem=csend.at[d], recv_sem=crecv.at[d],
            device_id={"fibre": to}, device_id_type=MESH))
    for c in spread:
        c.start()

    d_halo.wait_recv(0)
    do_d_records(dp, big.at[3], g, drec, last * TILE)
    do_d_records(dp, big.at[3], g, drec, 0)
    for d in range(1, nf):
        source = lax.rem(fi - d + nf, nf)
        pltpu.make_async_remote_copy(
            src_ref=planes.at[source], dst_ref=planes.at[source], send_sem=csend.at[d], recv_sem=crecv.at[d],
            device_id={"fibre": source}, device_id_type=MESH).wait_recv()
    total = planes[0]
    for i in range(1, nf):
        total = total + planes[i]
    gathered[core, me] = padded(total * factor).astype(BF)
    def piece(which, part, to):
        return pltpu.make_async_remote_copy(
            src_ref=gathered.at[which, part], dst_ref=gathered.at[which, part], send_sem=esend.at[to],
            recv_sem=erecv.at[part], device_id=member(to), device_id_type=MESH)

    pl.when(me != 0)(piece(core, me, 0).start)
    for d in offsets:
        to = moved(d, 1)
        pl.when(to != 0)(piece(core, me, to).start)

    for i in range(CHUNKS):
        h_halo.wait_recv(i)
        do_mixed(h, big.at[2], x, mix, [(p, SPANS[i]) for p in EDGES])

    for s in range(members):
        pl.when(me != s)(piece(core, s, me).wait_recv)

    def forward(which):
        return pltpu.make_async_remote_copy(
            src_ref=gathered.at[which], dst_ref=gathered.at[which], send_sem=fsem.at[0],
            recv_sem=fsem.at[1], device_id=partner, device_id_type=MESH)

    forward(core).start()
    forward(1 - core).wait_recv()

    forward(core).wait_send()
    swap.wait_send()
    for c in (*scatter, *spread):
        c.wait_send()
    for s in range(members):
        pl.when(me != s)(piece(core, me, s).wait_send)
    for halo, count in ((g_halo, CHUNKS), (h_halo, CHUNKS), (x_halo, 1), (d_halo, 1)):
        for i in range(count):
            halo.wait_send(i)


def shards(factor, records, time_weight, fibre_weight, cotangent):
    nf, nt, nr = lax.axis_size("fibre"), lax.axis_size("tm"), lax.axis_size("rep")
    members = (nt // 2) * nr
    used = 9 * (128 // members)
    height = -(-used // 16) * 16
    dma = pltpu.SemaphoreType.DMA
    any_space = pl.BlockSpec(memory_space=pl.ANY)
    mix, drec, gathered = pl.pallas_call(
        functools.partial(kernel, factor),
        out_shape=(
            pltpu.VMEM((16, 512, 128), BF), pltpu.VMEM((16, 512, 128), BF), pltpu.VMEM((2, members, height, 128), BF)
        ),
        in_specs=[pl.BlockSpec(memory_space=pltpu.HBM)] * 4,
        out_specs=(pl.BlockSpec(memory_space=pltpu.VMEM),) * 3,
        scratch_shapes=[
            pltpu.VMEM((16, 512, 128), BF),
            pltpu.VMEM((24, 512, 128), BF),
            pltpu.VMEM((24, 512, 128), BF),
            pltpu.VMEM((36, 128, 256), BF),
            pltpu.VMEM((36, 256, 128), BF),
            pltpu.VMEM((12, 256, 512), BF),
            pltpu.VMEM((36, 128, 256), BF),
            pltpu.VMEM((32, 128, 256), F32),
            pltpu.VMEM((2, 9, 128, 128), BF),
            pltpu.VMEM((4, 1280, 256), BF),
            pltpu.VMEM((2, 1280, 256), F32),
            pltpu.VMEM((2, 9, 128, 128), F32),
            pltpu.VMEM((9, 128, 128), F32),
            pltpu.VMEM((members, height, 128), WIRE),
            pltpu.VMEM((members, height, 128), WIRE),
            pltpu.VMEM((nf, used, 128), F32),
            dma((8,)),
            dma((2, CHUNKS)), dma((2, CHUNKS)), dma((2, CHUNKS)), dma((2, CHUNKS)),
            dma((2, 1)), dma((2, 1)), dma((2, 1)), dma((2, 1)),
            dma((2,)), dma((members,)), dma((members,)), dma((nf,)), dma((nf,)), dma((members,)), dma((members,)),
            dma((2,)),
        ],
        compiler_params=pltpu.CompilerParams(
            collective_id=0, has_side_effects=True, vmem_limit_bytes=48 << 20
        ),
        cost_estimate=pl.CostEstimate(flops=16 * 10**9, bytes_accessed=10**7, transcendentals=10**6),
        name="block",
    )(*(pltpu.with_memory_space_constraint(a, pltpu.HBM) for a in (records[0], time_weight, fibre_weight, cotangent[0])))

    def store(mix, drec, gathered, mixed, d_records, grad_time, grad_fibre, staged, sem):
        copies = [pltpu.make_async_copy(mix, mixed, sem.at[0]), pltpu.make_async_copy(drec, d_records, sem.at[1])]
        for c in copies:
            c.start()
        rows = 128 // members
        for i, out in enumerate((grad_time, grad_fibre)):
            for s in range(members):
                staged[i, :, rows * s : rows * s + rows] = gathered[i, s].astype(F32)[:used].reshape(9, rows, 128)
            copies.append(pltpu.make_async_copy(staged.at[i], out, sem.at[2 + i]))
            copies[-1].start()
        for c in copies:
            c.wait()

    field = jax.ShapeDtypeStruct((16, 512, 128), BF)
    grad = jax.ShapeDtypeStruct((9, 128, 128), F32)
    mixed, d_records, grad_time, grad_fibre = pl.pallas_call(
        store,
        out_shape=(field, field, grad, grad),
        in_specs=[any_space, any_space, pl.BlockSpec(memory_space=pltpu.VMEM)],
        out_specs=(any_space,) * 4,
        scratch_shapes=[pltpu.VMEM((2, 9, 128, 128), F32), dma((4,))],
        compiler_params=pltpu.CompilerParams(vmem_limit_bytes=8 << 20),
        cost_estimate=pl.CostEstimate(flops=0, bytes_accessed=10**7, transcendentals=0),
        name="store",
    )(mix, drec, gathered)
    return mixed[None], d_records[None], grad_time, grad_fibre


def solution(mesh):
    spec = P("rep", "fibre", "tm", None)
    total = 8 * 64 * 2048
    return jax.shard_map(
        functools.partial(shards, float(total) ** -0.5),
        mesh=mesh,
        in_specs=(spec, P(), P(), spec),
        out_specs=(spec, spec, P(), P()),
        check_vma=False,
    )
```
